32 devices in a mesh: seq: 8 (over y, x, core), head: 4 (over z).
Axes of the slice: x: 2, y: 2, z: 4, core: 2. Of those that a mesh axis runs over, the one named last changes fastest.
Arguments:
- queries: bfloat16 [16384, 4096], P('seq', 'head'), may hold values from -2 to 2
- key_rows: bfloat16 [16384, 4096], P('seq', 'head'), may hold values from -2 to 2
- value_rows: bfloat16 [16384, 4096], P('seq', 'head'), may hold values from -128 to 128
- decay_log: float32 [32, 16384], P('head', 'seq'), may hold values from -0.8 to 0
- norm_gain: float32 [4096], P('head'), may hold values from 0.1 to 1.9
- page_owner: int32 [16], replicated, may hold values from 0 to 7, as said below
Outputs:
- attended: bfloat16 [16384, 4096], P('seq', 'head')
- page_cache: bfloat16 [40, 32, 128, 128], P('seq', 'head')
The draws below stay inside these ranges and needn't reach their ends.
Inputs may be any that keep to these rules, and one draw needn't show every extreme that they name: `page_owner`: the 2 pages p = i * 2 to (i + 1) * 2 - 1 have different owners for every i; no owner keeps more than 5 pages and one keeps exactly 5.
All inputs are finite; a program needn't handle non-finite values.
Results may differ from the reference program's by a relative error of at most 0.0042.
Values may be sent and summed in bfloat16 or wider, within the bound.
No kernel may reach another device: no remote copies, remote signals or barrier semaphores. Data moves between devices by JAX's collectives and lax.ppermute only.
A program may use at most 128 MiB of HBM per device.

```python
import math
import jax
import jax.numpy as jnp
from jax import lax

HDIM = 128
TOK_DEV = 2048
BLOCK = 512
PAGE = 1024
SLOTS = 5
HEADS = 32
TOKENS = 16384
PAGES_DEV = 2
PAGES = 16
CACHE_ROWS = 40


def draw_value_rows(key, part):
    first, second, third = jax.random.split(key, 3)
    heads_rank = jnp.arange(HEADS).astype(jnp.float32)
    base = jnp.clip(jax.random.normal(first, (TOKENS, HEADS, HDIM), jnp.float32), -4.0, 4.0)
    head_scale = 10.0 ** ((heads_rank + jax.random.uniform(second, (HEADS,), jnp.float32)) / HEADS)
    row_scale = 10.0 ** (0.5 * jax.random.uniform(third, (TOKENS, 1, 1), jnp.float32))
    return (base * head_scale[None, :, None] * row_scale).reshape(TOKENS, HEADS * HDIM).astype(jnp.bfloat16)


def draw_decay_log(key, part):
    every_key_row = jax.random.split(key, 7)
    fast_share = 0.5
    fast = jax.random.uniform(every_key_row[0], (HEADS, 1), jnp.float32) < fast_share
    fast_rate = jax.random.uniform(every_key_row[1], (HEADS, 1), jnp.float32, 1.0 / 50.0, 1.0 / 30.0)
    slow_rate = jax.random.uniform(every_key_row[2], (HEADS, 1), jnp.float32, 0.1, 0.4) / TOKENS
    decay_rate = jnp.where(fast, fast_rate, slow_rate)
    segments = TOKENS // TOK_DEV
    decay_multiplier = jnp.exp(jax.random.uniform(every_key_row[3], (HEADS, segments), jnp.float32, math.log(0.5), math.log(2.0)))
    decay_multiplier = jnp.repeat(decay_multiplier, TOK_DEV, axis=1)
    leading_location = jax.random.randint(every_key_row[4], (), 0, TOKENS)
    trailing_location = (leading_location + 1 + jax.random.randint(every_key_row[6], (), 0, TOKENS - 1)) % TOKENS
    spike_location = jnp.stack([leading_location, trailing_location])
    spike_depth = jax.random.uniform(every_key_row[5], (2,), jnp.float32, math.log(1.25), math.log(2.0))
    token_positions = jnp.arange(TOKENS)
    spike_events = jnp.sum(jnp.where(token_positions[None, :] == spike_location[:, None], spike_depth[:, None], 0.0), axis=0)
    return -(decay_rate * decay_multiplier + spike_events[None, :])


def draw_page_owner(key, part):
    first, second, third, fourth = jax.random.split(key, 4)
    owner_count = PAGES // PAGES_DEV
    hottest = jax.random.randint(first, (), 0, owner_count)
    ranking = jax.random.permutation(second, owner_count)
    hot_device = ranking < SLOTS
    hot_page = jax.random.randint(third, (owner_count,), 0, PAGES_DEV)
    offset = jax.random.randint(fourth, (), 0, owner_count - 1)
    device_ids = jnp.arange(owner_count)[:, None]
    page_ids = jnp.arange(PAGES_DEV)[None, :]
    others = (hottest + 1 + (device_ids + page_ids + offset) % (owner_count - 1)) % owner_count
    chosen = jnp.where(hot_device[:, None] & (page_ids == hot_page[:, None]), hottest, others)
    return chosen.reshape(PAGES).astype(jnp.int32)


def steps_of(rng, dims, shards, low, top_value):
    level, own = 1.0, jax.random.fold_in(rng, 6)
    for position, shards_of in shards:
        steps = jnp.exp(jax.random.uniform(jax.random.fold_in(own, position), (shards_of,), jnp.float32, low / len(shards), top_value / len(shards)))
        level = level * jnp.repeat(steps, dims[position] // shards_of).reshape([-1 if axis == position else 1 for axis in range(len(dims))])
    return level


def normal_values(rng, shape, width, reach, shards=(), dtype=jnp.bfloat16):
    array = width * jax.random.normal(rng, shape, jnp.float32)
    if shards:
        array = array * steps_of(rng, shape, shards, -0.22, 0.18)
    return jnp.clip(array, -reach, reach).astype(dtype)


def setup_inputs(seed: int = 0) -> dict:
    splits = jax.random.split(jax.random.key(seed), 7)
    queries = normal_values(splits[0], (TOKENS, HEADS * HDIM), 0.3, 2.0, ((0, 8), (1, 4)))
    key_rows = normal_values(splits[1], (TOKENS, HEADS * HDIM), 0.3, 2.0, ((0, 8), (1, 4)))
    value_rows = draw_value_rows(jax.random.fold_in(splits[6], 71), 0)
    decay_log = draw_decay_log(jax.random.fold_in(splits[6], 71), 0)
    norm_gain = jnp.clip(1.0 + 0.18 * jax.random.normal(splits[4], (HEADS * HDIM,), jnp.float32), 0.1, 1.9)
    page_owner = draw_page_owner(jax.random.fold_in(splits[6], 71), 0)
    return {"queries": queries, "key_rows": key_rows, "value_rows": value_rows, "decay_log": decay_log, "norm_gain": norm_gain, "page_owner": page_owner}


def block_terms(query_blk, key_blk, value_blk, cumulative, carry_state):
    length = cumulative.shape[1]
    token_positions = jnp.arange(length)
    causal = (token_positions[:, None] >= token_positions[None, :])[None]
    spread = cumulative[:, :, None] - cumulative[:, None, :]
    damping = jnp.where(causal, jnp.exp(jnp.where(causal, spread, 0.0)), 0.0)
    scores = jnp.einsum('thd,shd->hts', query_blk.astype(jnp.float32), key_blk.astype(jnp.float32))
    weights = (scores * damping).astype(jnp.bfloat16)
    inner_sum = jnp.einsum('hts,shd->thd', weights.astype(jnp.float32), value_blk.astype(jnp.float32))
    carried = jnp.einsum('thd,hde->the', query_blk.astype(jnp.float32), carry_state, precision=lax.Precision.HIGHEST)
    output = inner_sum + carried * jnp.exp(cumulative).T[:, :, None]
    scaled_keys = (key_blk.astype(jnp.float32) * jnp.exp(cumulative[:, -1:] - cumulative).T[:, :, None]).astype(jnp.bfloat16)
    update = jnp.einsum('shd,she->hde', scaled_keys.astype(jnp.float32), value_blk.astype(jnp.float32))
    new_state = jnp.exp(cumulative[:, -1])[:, None, None] * carry_state + update
    return (output, new_state)

def reference(queries, key_rows, value_rows, decay_log, norm_gain, page_owner):
    per_page = PAGE // BLOCK
    block_shape = (PAGES, per_page, BLOCK, HEADS, HDIM)
    query_all = queries.reshape(block_shape)
    key_all = key_rows.reshape(block_shape)
    value_all = value_rows.reshape(block_shape)
    decay_all = decay_log.reshape(HEADS, PAGES, per_page, BLOCK).transpose(1, 2, 0, 3)
    gain_grid = norm_gain.reshape(HEADS, HDIM)

    def block_step(carry_state, pieces):
        query_blk, key_blk, value_blk, decay_blk = pieces
        cumulative = jnp.cumsum(decay_blk, axis=1)
        output, new_state = block_terms(query_blk, key_blk, value_blk, cumulative, carry_state)
        mean_square = lax.optimization_barrier(jnp.mean(output * output, axis=(1, 2)))
        normed = output * lax.rsqrt(mean_square + 1e-06)[:, None, None] * gain_grid[None]
        return (new_state, normed.astype(jnp.bfloat16).reshape(BLOCK, HEADS * HDIM))

    def page_step(carry_state, pieces):
        carry_state, normed = lax.scan(block_step, carry_state, pieces)
        return (carry_state, (normed, carry_state.astype(jnp.bfloat16)))
    initial = jnp.zeros((HEADS, HDIM, HDIM), jnp.float32)
    final_state, (normed, snapshots) = lax.scan(page_step, initial, (query_all, key_all, value_all, decay_all))
    attended = normed.reshape(TOKENS, HEADS * HDIM)
    page_order = jnp.arange(PAGES)
    earlier = (page_owner[:, None] == page_owner[None, :]) & (page_order[None, :] < page_order[:, None])
    slot_index = lax.optimization_barrier(jnp.sum(earlier.astype(jnp.int32), axis=1))
    target = (page_owner * SLOTS + slot_index).astype(jnp.int32)
    page_cache = jnp.zeros((CACHE_ROWS, HEADS, HDIM, HDIM), jnp.bfloat16).at[target].set(snapshots)
    return (attended, page_cache)
```

```python
import functools
import math

import jax
import jax.numpy as jnp
from jax import lax
from jax.experimental import pallas as pl
from jax.experimental.pallas import tpu as pltpu
from jax.sharding import PartitionSpec as P

BLOCK = 512
PAGE = 1024
SLOTS = 5
TILE = 256
LOG2E = math.log2(math.e)
MIB = 1 << 20

NT = (((1,), (1,)), ((), ()))
TN = (((0,), (0,)), ((), ()))


def split3(x):
    high = x.astype(jnp.bfloat16)
    rest = x - high.astype(jnp.float32)
    middle = rest.astype(jnp.bfloat16)
    low = (rest - middle.astype(jnp.float32)).astype(jnp.bfloat16)
    return high, middle, low


def state_kernel(heads, key_ref, value_ref, decay_ref, cum_ref, states_ref, reached_ref, end_ref, mid_ref, state, reached, upper):
    blk = pl.program_id(0)
    count = pl.num_programs(0)
    length, width = key_ref.shape
    dim = width // heads

    @pl.when(blk == 0)
    def _():
        state[...] = jnp.zeros_like(state)
        reached[...] = jnp.zeros_like(reached)
        rows = lax.broadcasted_iota(jnp.int32, (length, length), 0)
        cols = lax.broadcasted_iota(jnp.int32, (length, length), 1)
        upper[...] = jnp.where(rows <= cols, 1.0, 0.0).astype(jnp.bfloat16)

    parts = jnp.concatenate(split3(decay_ref[...] * LOG2E), axis=0)
    sums = jnp.dot(parts, upper[...], preferred_element_type=jnp.float32)
    cum = sums[:heads] + sums[heads : 2 * heads] + sums[2 * heads :]
    cum_ref[...] = cum
    last = cum[:, length - 1 :]
    to_last = jnp.exp2(last - cum).T
    decay = jnp.exp2(jnp.broadcast_to(last, (heads, dim)))
    for pair in range(heads // 2):
        scaled = []
        for head in (2 * pair, 2 * pair + 1):
            keys = key_ref[:, head * dim : (head + 1) * dim].astype(jnp.float32)
            scaled.append((keys * to_last[:, head : head + 1]).astype(jnp.bfloat16))
        update = lax.dot_general(
            jnp.concatenate(scaled, axis=1),
            value_ref[:, 2 * pair * dim : 2 * (pair + 1) * dim],
            TN,
            preferred_element_type=jnp.float32,
        )
        for which, head in enumerate((2 * pair, 2 * pair + 1)):
            rows = slice(head * dim, (head + 1) * dim)
            cols = slice(which * dim, (which + 1) * dim)
            state[rows] = decay[head : head + 1] * state[rows] + update[cols, cols]
    reached[...] += jnp.broadcast_to(last, (heads, dim))
    states_ref[0] = state[...]
    reached_ref[0] = reached[...]
    size = heads * dim

    @pl.when(blk == PAGE // BLOCK - 1)
    def _():
        mid_ref[...] = state[...].astype(jnp.bfloat16)
        end_ref[size + 3 * heads :] = jnp.concatenate(split3(reached[...]), axis=0)

    @pl.when(blk == count - 1)
    def _():
        end_ref[:size] = state[...].astype(jnp.bfloat16)
        end_ref[size : size + 3 * heads] = jnp.concatenate(split3(reached[...]), axis=0)


def run_states(key_rows, value_rows, decay_log):
    tokens, width = key_rows.shape
    heads = decay_log.shape[0]
    dim = width // heads
    blocks = tokens // BLOCK
    size = heads * dim
    return pl.pallas_call(
        functools.partial(state_kernel, heads),
        grid=(blocks,),
        in_specs=[
            pl.BlockSpec((BLOCK, width), lambda b: (b, 0)),
            pl.BlockSpec((BLOCK, width), lambda b: (b, 0)),
            pl.BlockSpec((heads, BLOCK), lambda b: (0, b)),
        ],
        out_specs=[
            pl.BlockSpec((heads, BLOCK), lambda b: (0, b)),
            pl.BlockSpec((1, size, dim), lambda b: (b, 0, 0)),
            pl.BlockSpec((1, heads, dim), lambda b: (b, 0, 0)),
            pl.BlockSpec((size + 6 * heads, dim), lambda b: (0, 0)),
            pl.BlockSpec((size, dim), lambda b: (0, 0)),
        ],
        out_shape=[
            jax.ShapeDtypeStruct((heads, tokens), jnp.float32),
            jax.ShapeDtypeStruct((blocks, size, dim), jnp.float32),
            jax.ShapeDtypeStruct((blocks, heads, dim), jnp.float32),
            jax.ShapeDtypeStruct((size + 6 * heads, dim), jnp.bfloat16),
            jax.ShapeDtypeStruct((size, dim), jnp.bfloat16),
        ],
        scratch_shapes=[
            pltpu.VMEM((size, dim), jnp.float32),
            pltpu.VMEM((heads, dim), jnp.float32),
            pltpu.VMEM((BLOCK, BLOCK), jnp.bfloat16),
        ],
        compiler_params=pltpu.CompilerParams(vmem_limit_bytes=24 * MIB),
        cost_estimate=pl.CostEstimate(flops=4 * tokens * width * dim, bytes_accessed=4 * tokens * width, transcendentals=0),
        name="states",
    )(key_rows, value_rows, decay_log)


def inner_kernel(heads, query_ref, key_ref, value_ref, cum_ref, out_ref):
    length, width = query_ref.shape
    dim = width // heads
    cum = cum_ref[...]
    cum_cols = cum.T
    causal = lax.broadcasted_iota(jnp.int32, (TILE, TILE), 0) >= lax.broadcasted_iota(jnp.int32, (TILE, TILE), 1)
    for head in range(heads):
        lanes = slice(head * dim, (head + 1) * dim)
        for tile in range(length // TILE):
            start, stop = tile * TILE, (tile + 1) * TILE
            scores = lax.dot_general(
                query_ref[start:stop, lanes], key_ref[:stop, lanes], NT, preferred_element_type=jnp.float32
            )
            damping = jnp.exp2(cum_cols[start:stop, head : head + 1] - cum[head : head + 1, :stop])
            weights = scores * damping
            diagonal = jnp.where(causal, weights[:, start:], 0.0)
            if tile:
                weights = jnp.concatenate([weights[:, :start], diagonal], axis=1)
            else:
                weights = diagonal
            out_ref[start:stop, lanes] = jnp.dot(
                weights.astype(jnp.bfloat16), value_ref[:stop, lanes], preferred_element_type=jnp.float32
            )


def run_inner(queries, key_rows, value_rows, cumulative):
    tokens, width = queries.shape
    heads = cumulative.shape[0]
    rows = pl.BlockSpec((BLOCK, width), lambda b: (b, 0))
    return pl.pallas_call(
        functools.partial(inner_kernel, heads),
        grid=(tokens // BLOCK,),
        in_specs=[rows, rows, rows, pl.BlockSpec((heads, BLOCK), lambda b: (0, b))],
        out_specs=rows,
        out_shape=jax.ShapeDtypeStruct((tokens, width), jnp.float32),
        compiler_params=pltpu.CompilerParams(vmem_limit_bytes=32 * MIB),
        cost_estimate=pl.CostEstimate(flops=4 * tokens * width * BLOCK, bytes_accessed=10 * tokens * width, transcendentals=0),
        name="inner",
    )(queries, key_rows, value_rows, cumulative)


def read_logs(ends, size, heads):
    whole, first = [], []
    for end in ends:
        parts = end[size:].astype(jnp.float32)
        whole.append(parts[:heads] + parts[heads : 2 * heads] + parts[2 * heads : 3 * heads])
        first.append(parts[3 * heads : 4 * heads] + parts[4 * heads : 5 * heads] + parts[5 * heads :])
    return whole, first


def gather_states(total, ends, places, logs, place, extra, heads, dim):
    for source, end in enumerate(ends):

        @pl.when(places[source] < place)
        def _():
            log = extra
            for other, other_log in enumerate(logs):
                between = (places[other] > places[source]) & (places[other] < place)
                log = log + jnp.where(between, other_log, 0.0)
            factor = jnp.exp2(log)
            for head in range(heads):
                rows = slice(head * dim, (head + 1) * dim)
                total[rows] += factor[head : head + 1] * end[rows].astype(jnp.float32)


def finish_kernel(heads, index_ref, inner_ref, query_ref, cum_ref, states_ref, reached_ref, *refs):
    *ends, out_ref, square_ref, entry = refs
    blk = pl.program_id(0)
    length, width = query_ref.shape
    dim = width // heads
    size = heads * dim

    @pl.when(blk == 0)
    def _():
        place = index_ref[0]
        logs, _unused = read_logs(ends, size, heads)
        entry[...] = jnp.zeros_like(entry)
        places = [place ^ offset for offset in range(len(ends))]
        gather_states(entry, ends, places, logs, place, jnp.zeros((heads, dim), jnp.float32), heads, dim)

    started = blk > 0
    until = jnp.where(started, reached_ref[0], 0.0)
    factor = jnp.exp2(until)
    growth = jnp.exp2(cum_ref[...]).T
    squares = jnp.zeros((length, dim), jnp.float32)
    zero = jnp.zeros((dim, dim), jnp.bfloat16)
    for pair in range(heads // 2):
        highs, lows = [], []
        for head in (2 * pair, 2 * pair + 1):
            rows = slice(head * dim, (head + 1) * dim)
            state = factor[head : head + 1] * entry[rows] + jnp.where(started, states_ref[0, rows], 0.0)
            high = state.astype(jnp.bfloat16)
            highs.append(high)
            lows.append((state - high.astype(jnp.float32)).astype(jnp.bfloat16))
        query = query_ref[:, 2 * pair * dim : 2 * (pair + 1) * dim]
        carried = 0.0
        for one, two in (highs, lows):
            both = jnp.concatenate(
                [jnp.concatenate([one, zero], axis=1), jnp.concatenate([zero, two], axis=1)], axis=0
            )
            carried = carried + jnp.dot(query, both, preferred_element_type=jnp.float32)
        for which, head in enumerate((2 * pair, 2 * pair + 1)):
            lanes = slice(head * dim, (head + 1) * dim)
            out = inner_ref[:, lanes] + carried[:, which * dim : (which + 1) * dim] * growth[:, head : head + 1]
            out_ref[:, lanes] = out
            squares += out * out
    high = squares.astype(jnp.bfloat16)
    low = (squares - high.astype(jnp.float32)).astype(jnp.bfloat16)
    ones = jnp.ones((8, dim), jnp.bfloat16)
    sums = lax.dot_general(ones, high, NT, preferred_element_type=jnp.float32)
    sums = sums + lax.dot_general(ones, low, NT, preferred_element_type=jnp.float32)
    square_ref[0] = sums


def run_finish(index, inner, queries, cumulative, states, reached, ends):
    tokens, width = queries.shape
    heads = cumulative.shape[0]
    dim = width // heads
    size = heads * dim
    blocks = tokens // BLOCK
    rows = pl.BlockSpec((BLOCK, width), lambda b: (b, 0))
    before = lambda b: (jnp.maximum(b, 1) - 1, 0, 0)
    return pl.pallas_call(
        functools.partial(finish_kernel, heads),
        grid=(blocks,),
        in_specs=[
            pl.BlockSpec(memory_space=pltpu.SMEM),
            rows,
            rows,
            pl.BlockSpec((heads, BLOCK), lambda b: (0, b)),
            pl.BlockSpec((1, size, dim), before),
            pl.BlockSpec((1, heads, dim), before),
        ]
        + [pl.BlockSpec(end.shape, lambda b: (0, 0)) for end in ends],
        out_specs=[rows, pl.BlockSpec((1, 8, BLOCK), lambda b: (b, 0, 0))],
        out_shape=[
            jax.ShapeDtypeStruct((tokens, width), jnp.float32),
            jax.ShapeDtypeStruct((blocks, 8, BLOCK), jnp.float32),
        ],
        input_output_aliases={1: 0},
        scratch_shapes=[pltpu.VMEM((size, dim), jnp.float32)],
        compiler_params=pltpu.CompilerParams(vmem_limit_bytes=40 * MIB),
        cost_estimate=pl.CostEstimate(flops=4 * tokens * width * dim, bytes_accessed=10 * tokens * width, transcendentals=0),
        name="finish",
    )(index, inner, queries, cumulative, states, reached, *ends)


def scale_kernel(whole_width, out_ref, gain_ref, *refs):
    *squares, attended_ref = refs
    total = squares[0][0]
    for square in squares[1:]:
        total = total + square[0]
    scale = lax.rsqrt(total * (1.0 / whole_width) + 1e-06).T[:, :1]
    attended_ref[...] = (out_ref[...] * scale * gain_ref[...]).astype(jnp.bfloat16)


def run_scale(out, gain, squares, whole_width):
    tokens, width = out.shape
    rows = pl.BlockSpec((BLOCK, width), lambda b: (b, 0))
    return pl.pallas_call(
        functools.partial(scale_kernel, whole_width),
        grid=(tokens // BLOCK,),
        in_specs=[rows, pl.BlockSpec((1, width), lambda b: (0, 0))]
        + [pl.BlockSpec((1, 8, BLOCK), lambda b: (b, 0, 0)) for _ in squares],
        out_specs=rows,
        out_shape=jax.ShapeDtypeStruct((tokens, width), jnp.bfloat16),
        compiler_params=pltpu.CompilerParams(vmem_limit_bytes=24 * MIB),
        cost_estimate=pl.CostEstimate(flops=tokens * width, bytes_accessed=6 * tokens * width, transcendentals=0),
        name="scale",
    )(out, gain.reshape(1, width), *squares)


def cache_kernel(heads, count, index_ref, owner_ref, *refs):
    ends, mids = refs[:count], refs[count : 2 * count]
    cache_ref, total, logs_ref, first_ref, page_of = refs[2 * count :]
    size, dim = mids[0].shape
    place = index_ref[0]
    places = [place ^ offset for offset in range(count)]
    whole, first = read_logs(ends, size, heads)
    for source in range(count):
        logs_ref[source] = whole[source]
        first_ref[source] = first[source]
    for slot in range(SLOTS):
        page_of[slot] = -1

    def look(page, found):
        mine = owner_ref[page] == place

        @pl.when(mine)
        def _():
            page_of[found] = page

        return found + mine.astype(jnp.int32)

    lax.fori_loop(0, owner_ref.shape[0], look, jnp.int32(0))

    def fill(slot, carry):
        page = page_of[slot]
        total[...] = jnp.zeros_like(total)

        @pl.when(page >= 0)
        def _():
            at_end = page % 2 == 1
            until = page // 2 + page % 2
            logs = [logs_ref[source] for source in range(count)]
            extra = jnp.zeros((heads, dim), jnp.float32)
            for source in range(count):
                extra = extra + jnp.where((places[source] == until) & jnp.logical_not(at_end), first_ref[source], 0.0)
            gather_states(total, ends, places, logs, until, extra, heads, dim)
            for source in range(count):

                @pl.when((places[source] == until) & jnp.logical_not(at_end))
                def _():
                    total[...] += mids[source][...].astype(jnp.float32)

        cache_ref[slot] = total[...].astype(jnp.bfloat16)
        return carry

    lax.fori_loop(0, SLOTS, fill, 0)


def run_cache(index, page_owner, ends, mids, heads):
    size, dim = mids[0].shape
    count = len(ends)
    vmem = pl.BlockSpec(memory_space=pltpu.VMEM)
    smem = pl.BlockSpec(memory_space=pltpu.SMEM)
    return pl.pallas_call(
        functools.partial(cache_kernel, heads, count),
        in_specs=[smem, smem] + [vmem] * (2 * count),
        out_specs=vmem,
        out_shape=jax.ShapeDtypeStruct((SLOTS, size, dim), jnp.bfloat16),
        scratch_shapes=[
            pltpu.VMEM((size, dim), jnp.float32),
            pltpu.VMEM((count, heads, dim), jnp.float32),
            pltpu.VMEM((count, heads, dim), jnp.float32),
            pltpu.SMEM((SLOTS,), jnp.int32),
        ],
        compiler_params=pltpu.CompilerParams(vmem_limit_bytes=32 * MIB),
        cost_estimate=pl.CostEstimate(flops=20 * size * dim, bytes_accessed=20 * size * dim, transcendentals=0),
        name="cache",
    )(index, page_owner, *ends, *mids)


def swap(value, axis, offset):
    return lax.ppermute(value, axis, [(place, place ^ offset) for place in range(lax.axis_size(axis))])


def everyones(value, axis):
    count = lax.axis_size(axis)
    held = {0: value}
    for offset in range(2, count, 2):
        held[offset] = swap(value, axis, offset)
    for offset in range(0, count, 2):
        held[offset + 1] = swap(held[offset], axis, 1)
    return [held[offset] for offset in range(count)]


def shards(queries, key_rows, value_rows, decay_log, norm_gain, page_owner):
    heads = decay_log.shape[0]
    dim = queries.shape[1] // heads
    index = lax.axis_index("seq").astype(jnp.int32).reshape(1)
    cumulative, states, reached, end, mid = run_states(key_rows, value_rows, decay_log)
    ends = everyones(end, "seq")
    inner = run_inner(queries, key_rows, value_rows, cumulative)
    out, square = run_finish(index, inner, queries, cumulative, states, reached, ends)
    squares = [square] + [swap(square, "head", offset) for offset in range(1, lax.axis_size("head"))]
    mid, _ = lax.optimization_barrier((mid, ends[-1]))
    mids = everyones(mid, "seq")
    attended = run_scale(out, norm_gain, squares, queries.shape[1] * lax.axis_size("head"))
    page_cache = run_cache(index, page_owner, ends, mids, heads)
    return attended, page_cache.reshape(SLOTS, heads, dim, dim)


def solution(mesh):
    return jax.shard_map(
        shards,
        mesh=mesh,
        in_specs=(
            P("seq", "head"),
            P("seq", "head"),
            P("seq", "head"),
            P("head", "seq"),
            P("head"),
            P(),
        ),
        out_specs=(P("seq", "head"), P("seq", "head", None, None)),
        check_vma=False,
    )
```

```python
import functools
import math

import jax
import jax.numpy as jnp
from jax import lax
from jax.experimental import pallas as pl
from jax.experimental.pallas import tpu as pltpu
from jax.sharding import PartitionSpec as P

BLOCK = 512
PAGE = 1024
SLOTS = 5
TILE = 256
LOG2E = math.log2(math.e)
MIB = 1 << 20

NT = (((1,), (1,)), ((), ()))
TN = (((0,), (0,)), ((), ()))


def split3(x):
    high = x.astype(jnp.bfloat16)
    rest = x - high.astype(jnp.float32)
    middle = rest.astype(jnp.bfloat16)
    low = (rest - middle.astype(jnp.float32)).astype(jnp.bfloat16)
    return high, middle, low


def state_kernel(heads, key_ref, value_ref, decay_ref, cum_ref, states_ref, reached_ref, end_ref, mid_ref, reached, upper):
    blk = pl.program_id(0)
    count = pl.num_programs(0)
    length, width = key_ref.shape
    dim = width // heads
    size = heads * dim

    @pl.when(blk == 0)
    def _():
        reached[...] = jnp.zeros_like(reached)
        states_ref[count - 1] = jnp.zeros((size, dim), jnp.float32)
        rows = lax.broadcasted_iota(jnp.int32, (length, length), 0)
        cols = lax.broadcasted_iota(jnp.int32, (length, length), 1)
        upper[...] = jnp.where(rows <= cols, 1.0, 0.0).astype(jnp.bfloat16)

    parts = jnp.concatenate(split3(decay_ref[...] * LOG2E), axis=0)
    sums = jnp.dot(parts, upper[...], preferred_element_type=jnp.float32)
    cum = sums[:heads] + sums[heads : 2 * heads] + sums[2 * heads :]
    cum_ref[...] = cum
    last = cum[:, length - 1 :]
    to_last = jnp.exp2(last - cum)
    decay = jnp.exp2(jnp.broadcast_to(last, (heads, dim)))
    before = jnp.where(blk == 0, count, blk) - 1
    for pair in range(heads // 2):
        scaled = []
        for head in (2 * pair, 2 * pair + 1):
            keys = key_ref[:, head * dim : (head + 1) * dim].T.astype(jnp.float32)
            scaled.append((keys * to_last[head : head + 1]).astype(jnp.bfloat16))
        update = jnp.dot(
            jnp.concatenate(scaled, axis=0),
            value_ref[:, 2 * pair * dim : 2 * (pair + 1) * dim],
            preferred_element_type=jnp.float32,
        )
        for which, head in enumerate((2 * pair, 2 * pair + 1)):
            rows = slice(head * dim, (head + 1) * dim)
            cols = slice(which * dim, (which + 1) * dim)
            states_ref[blk, rows] = decay[head : head + 1] * states_ref[before, rows] + update[cols, cols]
    reached[...] += jnp.broadcast_to(last, (heads, dim))
    reached_ref[blk] = reached[...]

    @pl.when(blk == PAGE // BLOCK - 1)
    def _():
        mid_ref[...] = states_ref[blk].astype(jnp.bfloat16)
        end_ref[size + 3 * heads :] = jnp.concatenate(split3(reached[...]), axis=0)

    @pl.when(blk == count - 1)
    def _():
        end_ref[:size] = states_ref[blk].astype(jnp.bfloat16)
        end_ref[size : size + 3 * heads] = jnp.concatenate(split3(reached[...]), axis=0)


def in_hbm(value):
    return pltpu.with_memory_space_constraint(value, pltpu.HBM)


def run_states(key_rows, value_rows, decay_log):
    tokens, width = key_rows.shape
    heads = decay_log.shape[0]
    dim = width // heads
    blocks = tokens // BLOCK
    size = heads * dim
    whole = pl.BlockSpec(memory_space=pltpu.VMEM)
    return pl.pallas_call(
        functools.partial(state_kernel, heads),
        grid=(blocks,),
        in_specs=[
            pl.BlockSpec((BLOCK, width), lambda b: (b, 0)),
            pl.BlockSpec((BLOCK, width), lambda b: (b, 0)),
            pl.BlockSpec((heads, BLOCK), lambda b: (0, b)),
        ],
        out_specs=[pl.BlockSpec((heads, BLOCK), lambda b: (0, b)), whole, whole, whole, whole],
        out_shape=[
            jax.ShapeDtypeStruct((heads, tokens), jnp.float32),
            pltpu.VMEM((blocks, size, dim), jnp.float32),
            pltpu.VMEM((blocks, heads, dim), jnp.float32),
            pltpu.VMEM((size + 6 * heads, dim), jnp.bfloat16),
            pltpu.VMEM((size, dim), jnp.bfloat16),
        ],
        scratch_shapes=[
            pltpu.VMEM((heads, dim), jnp.float32),
            pltpu.VMEM((BLOCK, BLOCK), jnp.bfloat16),
        ],
        compiler_params=pltpu.CompilerParams(vmem_limit_bytes=12 * MIB),
        cost_estimate=pl.CostEstimate(flops=4 * tokens * width * dim, bytes_accessed=4 * tokens * width, transcendentals=0),
        name="states",
    )(in_hbm(key_rows), in_hbm(value_rows), decay_log)


def inner_kernel(heads, first, query_ref, key_ref, value_ref, cum_ref, *refs):
    out_ref, done_ref = refs[-2:]
    length, width = query_ref.shape
    dim = width // heads
    cum = cum_ref[...]
    cum_cols = cum.T
    causal = lax.broadcasted_iota(jnp.int32, (TILE, TILE), 0) >= lax.broadcasted_iota(jnp.int32, (TILE, TILE), 1)
    base = (pl.program_id(0) + first) * length
    for head in range(heads):
        lanes = slice(head * dim, (head + 1) * dim)
        for tile in range(length // TILE):
            start, stop = tile * TILE, (tile + 1) * TILE
            scores = lax.dot_general(
                query_ref[start:stop, lanes], key_ref[:stop, lanes], NT, preferred_element_type=jnp.float32
            )
            damping = jnp.exp2(cum_cols[start:stop, head : head + 1] - cum[head : head + 1, :stop])
            weights = scores * damping
            diagonal = jnp.where(causal, weights[:, start:], 0.0)
            if tile:
                weights = jnp.concatenate([weights[:, :start], diagonal], axis=1)
            else:
                weights = diagonal
            out_ref[pl.ds(pl.multiple_of(base + start, TILE), TILE), lanes] = jnp.dot(
                weights.astype(jnp.bfloat16), value_ref[:stop, lanes], preferred_element_type=jnp.float32
            )
    done_ref[...] = cum[:, :128]


def run_inner(queries, key_rows, value_rows, cumulative, first, count, earlier=None):
    tokens, width = queries.shape
    heads = cumulative.shape[0]
    rows = pl.BlockSpec((BLOCK, width), lambda b: (b + first, 0))
    whole = pl.BlockSpec(memory_space=pltpu.VMEM)
    share = tokens * count * BLOCK // tokens
    return pl.pallas_call(
        functools.partial(inner_kernel, heads, first),
        grid=(count,),
        in_specs=[rows, rows, rows, pl.BlockSpec((heads, BLOCK), lambda b: (0, b + first))]
        + ([] if earlier is None else [whole]),
        out_specs=[whole, pl.BlockSpec((heads, 128), lambda b: (0, 0))],
        out_shape=[pltpu.VMEM((tokens, width), jnp.float32), jax.ShapeDtypeStruct((heads, 128), jnp.float32)],
        input_output_aliases={} if earlier is None else {4: 0},
        compiler_params=pltpu.CompilerParams(vmem_limit_bytes=12 * MIB),
        cost_estimate=pl.CostEstimate(flops=4 * share * width * BLOCK, bytes_accessed=10 * share * width, transcendentals=0),
        name="inner",
    )(in_hbm(queries), in_hbm(key_rows), in_hbm(value_rows), cumulative, *([] if earlier is None else [earlier]))


def read_logs(ends, size, heads):
    whole, first = [], []
    for end in ends:
        parts = end[size:].astype(jnp.float32)
        whole.append(parts[:heads] + parts[heads : 2 * heads] + parts[2 * heads : 3 * heads])
        first.append(parts[3 * heads : 4 * heads] + parts[4 * heads : 5 * heads] + parts[5 * heads :])
    return whole, first


def gather_states(total, ends, places, logs, place, extra, heads, dim):
    factors = []
    for source in range(len(ends)):
        log = extra
        for other, other_log in enumerate(logs):
            between = (places[other] > places[source]) & (places[other] < place)
            log = log + jnp.where(between, other_log, 0.0)
        factors.append(jnp.where(places[source] < place, jnp.exp2(log), 0.0))
    for head in range(heads):
        rows = slice(head * dim, (head + 1) * dim)
        value = jnp.zeros((dim, dim), jnp.float32)
        for source, end in enumerate(ends):
            value += factors[source][head : head + 1] * end[rows].astype(jnp.float32)
        total[rows] = value


def finish_kernel(heads, inner_ref, query_ref, cum_ref, states_ref, reached_ref, *refs):
    *ends, out_ref, square_ref, entry = refs
    blk = pl.program_id(0)
    length, width = query_ref.shape
    dim = width // heads
    size = heads * dim

    @pl.when(blk == 0)
    def _():
        place = lax.axis_index("seq")
        logs, _unused = read_logs(ends, size, heads)
        places = [place ^ offset for offset in range(len(ends))]
        gather_states(entry, ends, places, logs, place, jnp.zeros((heads, dim), jnp.float32), heads, dim)

    started = blk > 0
    before = jnp.maximum(blk, 1) - 1
    factor = jnp.exp2(jnp.where(started, reached_ref[before], 0.0))
    growth = jnp.exp2(cum_ref[...]).T
    squares = jnp.zeros((length, dim), jnp.float32)
    zero = jnp.zeros((dim, dim), jnp.bfloat16)
    here = pl.ds(pl.multiple_of(blk * length, length), length)
    for pair in range(heads // 2):
        highs, lows = [], []
        for head in (2 * pair, 2 * pair + 1):
            rows = slice(head * dim, (head + 1) * dim)
            state = factor[head : head + 1] * entry[rows] + jnp.where(started, states_ref[before, rows], 0.0)
            high = state.astype(jnp.bfloat16)
            highs.append(high)
            lows.append((state - high.astype(jnp.float32)).astype(jnp.bfloat16))
        query = query_ref[:, 2 * pair * dim : 2 * (pair + 1) * dim]
        carried = 0.0
        for one, two in (highs, lows):
            both = jnp.concatenate(
                [jnp.concatenate([one, zero], axis=1), jnp.concatenate([zero, two], axis=1)], axis=0
            )
            carried = carried + jnp.dot(query, both, preferred_element_type=jnp.float32)
        for which, head in enumerate((2 * pair, 2 * pair + 1)):
            lanes = slice(head * dim, (head + 1) * dim)
            out = inner_ref[here, lanes] + carried[:, which * dim : (which + 1) * dim] * growth[:, head : head + 1]
            out_ref[here, lanes] = out
            squares += out * out
    high = squares.astype(jnp.bfloat16)
    low = (squares - high.astype(jnp.float32)).astype(jnp.bfloat16)
    ones = jnp.ones((8, dim), jnp.bfloat16)
    sums = lax.dot_general(ones, high, NT, preferred_element_type=jnp.float32)
    sums = sums + lax.dot_general(ones, low, NT, preferred_element_type=jnp.float32)
    for row in range(length // 128):
        square_ref[pl.ds(blk * (length // 128) + row, 1)] = sums[:1, row * 128 : (row + 1) * 128]


def run_finish(inner, queries, cumulative, states, reached, ends):
    tokens, width = queries.shape
    heads = cumulative.shape[0]
    dim = width // heads
    size = heads * dim
    blocks = tokens // BLOCK
    rows = pl.BlockSpec((BLOCK, width), lambda b: (b, 0))
    whole = pl.BlockSpec(memory_space=pltpu.VMEM)
    return pl.pallas_call(
        functools.partial(finish_kernel, heads),
        grid=(blocks,),
        in_specs=[
            whole,
            rows,
            pl.BlockSpec((heads, BLOCK), lambda b: (0, b)),
            whole,
            whole,
        ]
        + [whole] * len(ends),
        out_specs=[whole, whole],
        out_shape=[
            pltpu.VMEM((tokens, width), jnp.float32),
            pltpu.VMEM((tokens // 128, 128), jnp.float32),
        ],
        input_output_aliases={0: 0},
        scratch_shapes=[pltpu.VMEM((size, dim), jnp.float32)],
        compiler_params=pltpu.CompilerParams(vmem_limit_bytes=12 * MIB),
        cost_estimate=pl.CostEstimate(flops=4 * tokens * width * dim, bytes_accessed=10 * tokens * width, transcendentals=0),
        name="finish",
    )(inner, in_hbm(queries), cumulative, states, reached, *ends)


def scale_kernel(whole_width, out_ref, gain_ref, *refs):
    *squares, attended_ref = refs
    blk = pl.program_id(0)
    length, width = attended_ref.shape
    for part in range(length // 128):
        row = pl.ds(blk * (length // 128) + part, 1)
        total = squares[0][row]
        for square in squares[1:]:
            total = total + square[row]
        scale = lax.rsqrt(total * (1.0 / whole_width) + 1e-06)
        scale = jnp.broadcast_to(scale, (8, 128)).T[:, :1]
        here = pl.ds(pl.multiple_of(blk * length + part * 128, 128), 128)
        attended_ref[part * 128 : (part + 1) * 128] = (out_ref[here] * scale * gain_ref[...]).astype(jnp.bfloat16)


def run_scale(out, gain, squares, whole_width):
    tokens, width = out.shape
    whole = pl.BlockSpec(memory_space=pltpu.VMEM)
    return pl.pallas_call(
        functools.partial(scale_kernel, whole_width),
        grid=(tokens // BLOCK,),
        in_specs=[whole, whole] + [whole for _ in squares],
        out_specs=pl.BlockSpec((BLOCK, width), lambda b: (b, 0)),
        out_shape=jax.ShapeDtypeStruct((tokens, width), jnp.bfloat16),
        compiler_params=pltpu.CompilerParams(vmem_limit_bytes=12 * MIB),
        cost_estimate=pl.CostEstimate(flops=tokens * width, bytes_accessed=6 * tokens * width, transcendentals=0),
        name="scale",
    )(out, gain.reshape(1, width), *squares)


def cache_kernel(heads, count, owner_ref, *refs):
    ends, mids = refs[:count], refs[count : 2 * count]
    cache_ref, total, logs_ref, first_ref, page_of = refs[2 * count :]
    size, dim = mids[0].shape
    place = lax.axis_index("seq")
    places = [place ^ offset for offset in range(count)]
    whole, first = read_logs(ends, size, heads)
    for source in range(count):
        logs_ref[source] = whole[source]
        first_ref[source] = first[source]
    for slot in range(SLOTS):
        page_of[slot] = -1

    def look(page, found):
        mine = (owner_ref[page] == place) & (found < SLOTS)

        @pl.when(mine)
        def _():
            page_of[found] = page

        return found + mine.astype(jnp.int32)

    lax.fori_loop(0, owner_ref.shape[0], look, jnp.int32(0))

    def fill(slot, carry):
        page = page_of[slot]
        at_end = page % 2 == 1
        until = page // 2 + page % 2
        halfway = jnp.logical_not(at_end) & (page >= 0)

        @pl.when(page >= 0)
        def _():
            logs = [logs_ref[source] for source in range(count)]
            extra = jnp.zeros((heads, dim), jnp.float32)
            for source in range(count):
                extra = extra + jnp.where((places[source] == until) & halfway, first_ref[source], 0.0)
            gather_states(total, ends, places, logs, until, extra, heads, dim)

        @pl.when(page < 0)
        def _():
            total[...] = jnp.zeros_like(total)

        for source in range(count):

            @pl.when((places[source] == until) & halfway)
            def _():
                total[...] += mids[source][...].astype(jnp.float32)

        cache_ref[slot] = total[...].astype(jnp.bfloat16)
        return carry

    lax.fori_loop(0, SLOTS, fill, 0)


def run_cache(page_owner, ends, mids, heads):
    size, dim = mids[0].shape
    count = len(ends)
    vmem = pl.BlockSpec(memory_space=pltpu.VMEM)
    smem = pl.BlockSpec(memory_space=pltpu.SMEM)
    return pl.pallas_call(
        functools.partial(cache_kernel, heads, count),
        in_specs=[smem] + [vmem] * (2 * count),
        out_specs=vmem,
        out_shape=jax.ShapeDtypeStruct((SLOTS, size, dim), jnp.bfloat16),
        scratch_shapes=[
            pltpu.VMEM((size, dim), jnp.float32),
            pltpu.VMEM((count, heads, dim), jnp.float32),
            pltpu.VMEM((count, heads, dim), jnp.float32),
            pltpu.SMEM((SLOTS,), jnp.int32),
        ],
        compiler_params=pltpu.CompilerParams(vmem_limit_bytes=12 * MIB),
        cost_estimate=pl.CostEstimate(flops=20 * size * dim, bytes_accessed=20 * size * dim, transcendentals=0),
        name="cache",
    )(page_owner, *ends, *mids)


def swap(value, axis, offset):
    return lax.ppermute(value, axis, [(place, place ^ offset) for place in range(lax.axis_size(axis))])


def tie(value, *after):
    return lax.optimization_barrier((value, *after))[0]


def shards(queries, key_rows, value_rows, decay_log, norm_gain, page_owner):
    tokens, width = queries.shape
    heads = decay_log.shape[0]
    dim = width // heads
    count = lax.axis_size("seq")
    blocks = tokens // BLOCK
    cumulative, states, reached, end, mid = run_states(key_rows, value_rows, decay_log)
    ends, mids = {0: end}, {0: mid}
    for offset in range(2, count, 2):
        ends[offset] = swap(end, "seq", offset)
    ends[1] = swap(end, "seq", 1)
    inner, done = run_inner(queries, key_rows, value_rows, cumulative, 0, blocks // 2)
    mid = tie(mid, done)
    for offset in range(2, count, 2):
        mids[offset] = swap(mid, "seq", offset)
    inner, done = run_inner(queries, key_rows, value_rows, cumulative, blocks // 2, blocks - blocks // 2, inner)
    for offset in range(2, count, 2):
        ends[offset + 1] = swap(tie(ends[offset], done), "seq", 1)
    ends = [ends[offset] for offset in range(count)]
    out, square = run_finish(inner, queries, cumulative, states, reached, ends)
    squares = [square] + [swap(square, "head", offset) for offset in range(1, lax.axis_size("head"))]
    for offset in range(0, count, 2):
        mids[offset + 1] = swap(tie(mids[offset], square), "seq", 1)
    mids = [mids[offset] for offset in range(count)]
    attended = run_scale(out, norm_gain, squares, width * lax.axis_size("head"))
    page_cache = run_cache(page_owner, ends, mids, heads)
    return attended, page_cache.reshape(SLOTS, heads, dim, dim)


def solution(mesh):
    return jax.shard_map(
        shards,
        mesh=mesh,
        in_specs=(
            P("seq", "head"),
            P("seq", "head"),
            P("seq", "head"),
            P("head", "seq"),
            P("head"),
            P(),
        ),
        out_specs=(P("seq", "head"), P("seq", "head", None, None)),
        check_vma=False,
    )
```

```python
import functools
import math

import jax
import jax.numpy as jnp
from jax import lax
from jax.experimental import pallas as pl
from jax.experimental.pallas import tpu as pltpu
from jax.sharding import PartitionSpec as P

BLOCK = 512
PAGE = 1024
SLOTS = 5
TILE = 256
LOG2E = math.log2(math.e)
MIB = 1 << 20
SMALL = pl.CostEstimate(flops=1, bytes_accessed=1, transcendentals=0)

NT = (((1,), (1,)), ((), ()))
TN = (((0,), (0,)), ((), ()))


def split3(x):
    high = x.astype(jnp.bfloat16)
    rest = x - high.astype(jnp.float32)
    middle = rest.astype(jnp.bfloat16)
    low = (rest - middle.astype(jnp.float32)).astype(jnp.bfloat16)
    return high, middle, low


def state_kernel(heads, key_hbm, value_hbm, decay_hbm, cum_ref, states_ref, reached_ref, end_ref, mid_ref, keys, values, decays, sems):
    tokens, width = keys.shape
    dim = width // heads
    size = heads * dim
    blocks = tokens // BLOCK
    decay_copy = pltpu.make_async_copy(decay_hbm, decays, sems.at[2 * blocks])
    decay_copy.start()
    copies = []
    for blk in range(blocks):
        rows = pl.ds(blk * BLOCK, BLOCK)
        copies.append(
            (
                pltpu.make_async_copy(key_hbm.at[rows], keys.at[rows], sems.at[2 * blk]),
                pltpu.make_async_copy(value_hbm.at[rows], values.at[rows], sems.at[2 * blk + 1]),
            )
        )
        copies[-1][0].start()
        copies[-1][1].start()
    upper = jnp.where(
        lax.broadcasted_iota(jnp.int32, (BLOCK, BLOCK), 0) <= lax.broadcasted_iota(jnp.int32, (BLOCK, BLOCK), 1), 1.0, 0.0
    ).astype(jnp.bfloat16)
    decay_copy.wait()
    parts = [
        part for blk in range(blocks) for part in split3(decays[:, blk * BLOCK : (blk + 1) * BLOCK] * LOG2E)
    ]
    sums = jnp.dot(jnp.concatenate(parts, axis=0), upper, preferred_element_type=jnp.float32)
    to_last, decay = [], []
    reached = jnp.zeros((heads, dim), jnp.float32)
    for blk in range(blocks):
        base = 3 * heads * blk
        cum = sums[base : base + heads] + sums[base + heads : base + 2 * heads] + sums[base + 2 * heads : base + 3 * heads]
        cum_ref[:, blk * BLOCK : (blk + 1) * BLOCK] = cum
        last = cum[:, BLOCK - 1 :]
        to_last.append(jnp.exp2(last - cum))
        wide = jnp.broadcast_to(last, (heads, dim))
        decay.append(jnp.exp2(wide))
        reached = reached + wide
        reached_ref[blk] = reached
        if blk == PAGE // BLOCK - 1:
            end_ref[size + 3 * heads :] = jnp.concatenate(split3(reached), axis=0)
    end_ref[size : size + 3 * heads] = jnp.concatenate(split3(reached), axis=0)
    for blk in range(blocks):
        copies[blk][0].wait()
        copies[blk][1].wait()
        here = slice(blk * BLOCK, (blk + 1) * BLOCK)
        for pair in range(heads // 2):
            scaled = []
            for head in (2 * pair, 2 * pair + 1):
                turned = keys[here, head * dim : (head + 1) * dim].T.astype(jnp.float32)
                scaled.append((turned * to_last[blk][head : head + 1]).astype(jnp.bfloat16))
            update = jnp.dot(
                jnp.concatenate(scaled, axis=0),
                values[here, 2 * pair * dim : 2 * (pair + 1) * dim],
                preferred_element_type=jnp.float32,
            )
            for which, head in enumerate((2 * pair, 2 * pair + 1)):
                rows = slice(head * dim, (head + 1) * dim)
                cols = slice(which * dim, (which + 1) * dim)
                state = update[cols, cols]
                if blk:
                    state = state + decay[blk][head : head + 1] * states_ref[blk - 1, rows]
                states_ref[blk, rows] = state
                if blk == PAGE // BLOCK - 1:
                    mid_ref[rows] = state.astype(jnp.bfloat16)
                if blk == blocks - 1:
                    end_ref[rows] = state.astype(jnp.bfloat16)


def in_hbm(value):
    return pltpu.with_memory_space_constraint(value, pltpu.HBM)


HBM = pl.BlockSpec(memory_space=pltpu.HBM)
VMEM = pl.BlockSpec(memory_space=pltpu.VMEM)
SMEM = pl.BlockSpec(memory_space=pltpu.SMEM)


def run_states(key_rows, value_rows, decay_log):
    tokens, width = key_rows.shape
    heads = decay_log.shape[0]
    dim = width // heads
    blocks = tokens // BLOCK
    size = heads * dim
    return pl.pallas_call(
        functools.partial(state_kernel, heads),
        in_specs=[HBM] * 3,
        out_specs=[VMEM] * 7,
        out_shape=[
            pltpu.VMEM((heads, tokens), jnp.float32),
            pltpu.VMEM((blocks, size, dim), jnp.float32),
            pltpu.VMEM((blocks, heads, dim), jnp.float32),
            pltpu.VMEM((size + 6 * heads, dim), jnp.bfloat16),
            pltpu.VMEM((size, dim), jnp.bfloat16),
            pltpu.VMEM((tokens, width), jnp.bfloat16),
            pltpu.VMEM((tokens, width), jnp.bfloat16),
        ],
        scratch_shapes=[pltpu.VMEM((heads, tokens), jnp.float32), pltpu.SemaphoreType.DMA((2 * blocks + 1,))],
        compiler_params=pltpu.CompilerParams(vmem_limit_bytes=8 * MIB),
        cost_estimate=SMALL,
        name="states",
    )(in_hbm(key_rows), in_hbm(value_rows), in_hbm(decay_log))


def pair_of(one, two):
    zero = jnp.zeros_like(one)
    return jnp.concatenate([jnp.concatenate([one, zero], axis=1), jnp.concatenate([zero, two], axis=1)], axis=0)


def inner_kernel(heads, first, keys, values, cum_ref, states_ref, reached_ref, *refs):
    blk = pl.program_id(0) + first
    if first:
        queries, _, _, out_ref, growth_ref, done_ref = refs
    else:
        query_hbm, out_ref, growth_ref, done_ref, queries, sems = refs
        blocks = queries.shape[0] // BLOCK

        def copy_of(part):
            rows = pl.ds(part * BLOCK, BLOCK)
            return pltpu.make_async_copy(query_hbm.at[rows], queries.at[rows], sems.at[part])

        @pl.when(blk == 0)
        def _():
            for part in range(blocks):
                copy_of(part).start()
            copy_of(0).wait()

        @pl.when(blk == 1)
        def _():
            for part in range(1, blocks):
                copy_of(part).wait()

    tokens, width = queries.shape
    dim = width // heads
    base = pl.multiple_of(blk * BLOCK, BLOCK)
    cum = cum_ref[:, pl.ds(base, BLOCK)]
    cum_cols = cum.T
    before = jnp.maximum(blk, 1) - 1
    reached = jnp.where(blk > 0, reached_ref[before], 0.0)
    causal = lax.broadcasted_iota(jnp.int32, (TILE, TILE), 0) >= lax.broadcasted_iota(jnp.int32, (TILE, TILE), 1)
    items = [(head, tile) for head in range(heads) for tile in range(BLOCK // TILE)]

    def rows_of(start, count):
        return pl.ds(pl.multiple_of(base + start, TILE), count)

    def scores_of(head, tile):
        lanes = slice(head * dim, (head + 1) * dim)
        return lax.dot_general(
            queries[rows_of(tile * TILE, TILE), lanes],
            keys[rows_of(0, (tile + 1) * TILE), lanes],
            NT,
            preferred_element_type=jnp.float32,
        )

    def carried_of(pair, tile):
        states = []
        for head in (2 * pair, 2 * pair + 1):
            state = states_ref[before, head * dim : (head + 1) * dim]
            states.append(jnp.where(blk > 0, state, 0.0).astype(jnp.bfloat16))
        query = queries[rows_of(tile * TILE, TILE), 2 * pair * dim : 2 * (pair + 1) * dim]
        return jnp.dot(query, pair_of(*states), preferred_element_type=jnp.float32)

    scores = scores_of(*items[0])
    carried = {}
    for number, (head, tile) in enumerate(items):
        ahead = scores_of(*items[number + 1]) if number + 1 < len(items) else None
        if head % 2 == 0:
            carried[tile] = carried_of(head // 2, tile)
        lanes = slice(head * dim, (head + 1) * dim)
        start, stop = tile * TILE, (tile + 1) * TILE
        column = jnp.broadcast_to(cum_cols[start:stop, head : head + 1], (TILE, dim))
        columns = jnp.concatenate([column] * (stop // dim), axis=1)
        weights = scores * jnp.exp2(columns - cum[head : head + 1, :stop])
        diagonal = jnp.where(causal, weights[:, start:], 0.0)
        weights = jnp.concatenate([weights[:, :start], diagonal], axis=1) if tile else diagonal
        local = jnp.dot(
            weights.astype(jnp.bfloat16), values[rows_of(0, stop), lanes], preferred_element_type=jnp.float32
        )
        which = head % 2
        local = local + carried[tile][:, which * dim : (which + 1) * dim] * jnp.exp2(column)
        out_ref[rows_of(start, TILE), lanes] = local
        growth_ref[rows_of(start, TILE), lanes] = jnp.exp2(column + reached[head : head + 1])
        scores = ahead
    done_ref[...] = cum[:, :128]


def run_inner(keys, values, cumulative, states, reached, first, count, queries, earlier=()):
    tokens, width = keys.shape
    heads = cumulative.shape[0]
    share = count * BLOCK
    made = pltpu.VMEM((tokens, width), jnp.float32)
    out_shape = [made, made, pltpu.VMEM((heads, 128), jnp.float32)]
    if not first:
        out_shape.append(pltpu.VMEM((tokens, width), jnp.bfloat16))
        queries = in_hbm(queries)
    return pl.pallas_call(
        functools.partial(inner_kernel, heads, first),
        grid=(count,),
        in_specs=[VMEM] * 5 + [VMEM if first else HBM] + [VMEM] * len(earlier),
        out_specs=[VMEM] * len(out_shape),
        out_shape=out_shape,
        scratch_shapes=[] if first else [pltpu.SemaphoreType.DMA((tokens // BLOCK,))],
        input_output_aliases={6: 0, 7: 1} if first else {},
        compiler_params=pltpu.CompilerParams(vmem_limit_bytes=8 * MIB),
        cost_estimate=SMALL,
        name="inner",
    )(keys, values, cumulative, states, reached, queries, *earlier)


def read_logs(ends, size, heads):
    whole, first = [], []
    for end in ends:
        parts = end[size:].astype(jnp.float32)
        whole.append(parts[:heads] + parts[heads : 2 * heads] + parts[2 * heads : 3 * heads])
        first.append(parts[3 * heads : 4 * heads] + parts[4 * heads : 5 * heads] + parts[5 * heads :])
    return whole, first


def gather_states(total, ends, places, logs, place, extra, heads, dim):
    factors = []
    for source in range(len(ends)):
        log = extra
        for other, other_log in enumerate(logs):
            between = (places[other] > places[source]) & (places[other] < place)
            log = log + jnp.where(between, other_log, 0.0)
        factors.append(jnp.where(places[source] < place, jnp.exp2(log), 0.0))
    for head in range(heads):
        rows = slice(head * dim, (head + 1) * dim)
        value = jnp.zeros((dim, dim), jnp.float32)
        for source, end in enumerate(ends):
            value += factors[source][head : head + 1] * end[rows].astype(jnp.float32)
        total[rows] = value


def with_entry(heads, here, inner_ref, growth_ref, queries, entry, use):
    dim = entry.shape[1]
    for pair in range(heads // 2):
        rows = [slice(head * dim, (head + 1) * dim) for head in (2 * pair, 2 * pair + 1)]
        carried = jnp.dot(
            queries[here, 2 * pair * dim : 2 * (pair + 1) * dim],
            pair_of(entry[rows[0]], entry[rows[1]]),
            preferred_element_type=jnp.float32,
        )
        for which, lanes in enumerate(rows):
            part = carried[:, which * dim : (which + 1) * dim]
            use(2 * pair + which, inner_ref[here, lanes] + part * growth_ref[here, lanes])


def finish_kernel(heads, inner_ref, growth_ref, queries, *refs):
    *ends, square_ref, entry_ref, entry = refs
    blk = pl.program_id(0)
    tokens, width = queries.shape
    dim = width // heads
    size = heads * dim

    @pl.when(blk == 0)
    def _():
        place = lax.axis_index("seq")
        logs, _unused = read_logs(ends, size, heads)
        places = [place ^ offset for offset in range(len(ends))]
        gather_states(entry, ends, places, logs, place, jnp.zeros((heads, dim), jnp.float32), heads, dim)
        entry_ref[...] = entry[...].astype(jnp.bfloat16)

    total = [jnp.zeros((BLOCK, dim), jnp.float32)]

    def use(head, out):
        total[0] = total[0] + out * out

    here = pl.ds(pl.multiple_of(blk * BLOCK, BLOCK), BLOCK)
    with_entry(heads, here, inner_ref, growth_ref, queries, entry_ref, use)
    high = total[0].astype(jnp.bfloat16)
    low = (total[0] - high.astype(jnp.float32)).astype(jnp.bfloat16)
    ones = jnp.ones((8, dim), jnp.bfloat16)
    sums = lax.dot_general(ones, high, NT, preferred_element_type=jnp.float32)
    sums = sums + lax.dot_general(ones, low, NT, preferred_element_type=jnp.float32)
    for row in range(BLOCK // 128):
        square_ref[pl.ds(blk * (BLOCK // 128) + row, 1)] = sums[:1, row * 128 : (row + 1) * 128]


def run_finish(inner, growth, queries, ends, heads):
    tokens, width = queries.shape
    dim = width // heads
    size = heads * dim
    return pl.pallas_call(
        functools.partial(finish_kernel, heads),
        grid=(tokens // BLOCK,),
        in_specs=[VMEM] * (3 + len(ends)),
        out_specs=[VMEM, VMEM],
        out_shape=[pltpu.VMEM((tokens // 128, 128), jnp.float32), pltpu.VMEM((size, dim), jnp.bfloat16)],
        scratch_shapes=[pltpu.VMEM((size, dim), jnp.float32)],
        compiler_params=pltpu.CompilerParams(vmem_limit_bytes=8 * MIB),
        cost_estimate=SMALL,
        name="finish",
    )(inner, growth, queries, *ends)


def scale_kernel(heads, whole_width, inner_ref, growth_ref, queries, entry, gain_ref, *refs):
    *squares, attended_ref = refs
    blk = pl.program_id(0)
    length, width = attended_ref.shape
    dim = width // heads
    scales = []
    for part in range(length // 128):
        row = pl.ds(blk * (length // 128) + part, 1)
        total = squares[0][row]
        for square in squares[1:]:
            total = total + square[row]
        scale = lax.rsqrt(total * (1.0 / whole_width) + 1e-06)
        scales.append(jnp.broadcast_to(jnp.broadcast_to(scale, (8, 128)).T[:, :1], (128, dim)))
    scale = jnp.concatenate(scales, axis=0)

    def use(head, out):
        lanes = slice(head * dim, (head + 1) * dim)
        attended_ref[:, lanes] = (out * scale * gain_ref[:, lanes]).astype(jnp.bfloat16)

    here = pl.ds(pl.multiple_of(blk * length, length), length)
    with_entry(heads, here, inner_ref, growth_ref, queries, entry, use)


def run_scale(inner, growth, queries, entry, gain, squares, whole_width, heads):
    tokens, width = inner.shape
    return pl.pallas_call(
        functools.partial(scale_kernel, heads, whole_width),
        grid=(tokens // BLOCK,),
        in_specs=[VMEM] * (5 + len(squares)),
        out_specs=pl.BlockSpec((BLOCK, width), lambda b: (b, 0)),
        out_shape=jax.ShapeDtypeStruct((tokens, width), jnp.bfloat16),
        compiler_params=pltpu.CompilerParams(vmem_limit_bytes=8 * MIB),
        cost_estimate=SMALL,
        name="scale",
    )(inner, growth, queries, entry, gain.reshape(1, width), *squares)


def cache_kernel(heads, count, owner_ref, *refs):
    ends, mids = refs[:count], refs[count : 2 * count]
    cache_ref, total, logs_ref, first_ref, page_of = refs[2 * count :]
    size, dim = mids[0].shape
    place = lax.axis_index("seq")
    places = [place ^ offset for offset in range(count)]
    whole, first = read_logs(ends, size, heads)
    for source in range(count):
        logs_ref[source] = whole[source]
        first_ref[source] = first[source]
    for slot in range(SLOTS):
        page_of[slot] = -1

    def look(page, found):
        mine = (owner_ref[page] == place) & (found < SLOTS)

        @pl.when(mine)
        def _():
            page_of[found] = page

        return found + mine.astype(jnp.int32)

    lax.fori_loop(0, owner_ref.shape[0], look, jnp.int32(0))

    def fill(slot, carry):
        page = page_of[slot]
        at_end = page % 2 == 1
        until = page // 2 + page % 2
        halfway = jnp.logical_not(at_end) & (page >= 0)

        @pl.when(page >= 0)
        def _():
            logs = [logs_ref[source] for source in range(count)]
            extra = jnp.zeros((heads, dim), jnp.float32)
            for source in range(count):
                extra = extra + jnp.where((places[source] == until) & halfway, first_ref[source], 0.0)
            gather_states(total, ends, places, logs, until, extra, heads, dim)

        @pl.when(page < 0)
        def _():
            total[...] = jnp.zeros_like(total)

        for source in range(count):

            @pl.when((places[source] == until) & halfway)
            def _():
                total[...] += mids[source][...].astype(jnp.float32)

        cache_ref[slot] = total[...].astype(jnp.bfloat16)
        return carry

    lax.fori_loop(0, SLOTS, fill, 0)


def run_cache(page_owner, ends, mids, heads):
    size, dim = mids[0].shape
    count = len(ends)
    return pl.pallas_call(
        functools.partial(cache_kernel, heads, count),
        in_specs=[SMEM] + [VMEM] * (2 * count),
        out_specs=VMEM,
        out_shape=jax.ShapeDtypeStruct((SLOTS, size, dim), jnp.bfloat16),
        scratch_shapes=[
            pltpu.VMEM((size, dim), jnp.float32),
            pltpu.VMEM((count, heads, dim), jnp.float32),
            pltpu.VMEM((count, heads, dim), jnp.float32),
            pltpu.SMEM((SLOTS,), jnp.int32),
        ],
        compiler_params=pltpu.CompilerParams(vmem_limit_bytes=12 * MIB),
        cost_estimate=SMALL,
        name="cache",
    )(page_owner, *ends, *mids)


def swap(value, axis, offset):
    return lax.ppermute(value, axis, [(place, place ^ offset) for place in range(lax.axis_size(axis))])


def tie(value, *after):
    return lax.optimization_barrier((value, *after))[0]


def add_kernel(one_ref, two_ref, sum_ref):
    sum_ref[...] = one_ref[...] + two_ref[...]


def add(one, two):
    return pl.pallas_call(
        add_kernel,
        in_specs=[VMEM, VMEM],
        out_specs=VMEM,
        out_shape=pltpu.VMEM(one.shape, one.dtype),
        compiler_params=pltpu.CompilerParams(vmem_limit_bytes=4 * MIB),
        cost_estimate=SMALL,
        name="add",
    )(one, two)


def shards(queries, key_rows, value_rows, decay_log, norm_gain, page_owner):
    tokens, width = queries.shape
    heads = decay_log.shape[0]
    dim = width // heads
    count = lax.axis_size("seq")
    half = tokens // BLOCK // 2
    cumulative, states, reached, end, mid, keys, values = run_states(key_rows, value_rows, decay_log)
    local = (keys, values, cumulative, states, reached)
    ends, mids = {0: end}, {0: mid}
    for offset in range(2, count, 2):
        ends[offset] = swap(end, "seq", offset)
    ends[1] = swap(end, "seq", 1)
    mids[1] = swap(mid, "seq", 1)
    inner, growth, done, held = run_inner(*local, 0, half, queries)
    mid = tie(mid, done, ends[1], mids[1])
    for offset in range(2, count, 2):
        mids[offset] = swap(mid, "seq", offset)
    inner, growth, done = run_inner(*local, half, half, held, (inner, growth))
    for offset in range(2, count, 2):
        ends[offset + 1] = swap(tie(ends[offset], done), "seq", 1)
    ends = [ends[offset] for offset in range(count)]
    square, entry = run_finish(inner, growth, held, ends, heads)
    offset = 1
    while offset < lax.axis_size("head"):
        square = add(square, swap(square, "head", offset))
        offset *= 2
    for offset in range(2, count, 2):
        mids[offset + 1] = swap(tie(mids[offset], square), "seq", 1)
    mids = [mids[offset] for offset in range(count)]
    attended = run_scale(inner, growth, held, entry, norm_gain, [square], width * lax.axis_size("head"), heads)
    page_cache = run_cache(page_owner, ends, mids, heads)
    return attended, page_cache.reshape(SLOTS, heads, dim, dim)


def solution(mesh):
    return jax.shard_map(
        shards,
        mesh=mesh,
        in_specs=(
            P("seq", "head"),
            P("seq", "head"),
            P("seq", "head"),
            P("head", "seq"),
            P("head"),
            P(),
        ),
        out_specs=(P("seq", "head"), P("seq", "head", None, None)),
        check_vma=False,
    )
```

```python
import functools
import math

import jax
import jax.numpy as jnp
from jax import lax
from jax.experimental import pallas as pl
from jax.experimental.pallas import tpu as pltpu
from jax.sharding import PartitionSpec as P

BLOCK = 256
ROWS = 512
PAGE = 1024
SLOTS = 5
LOG2E = math.log2(math.e)
MIB = 1 << 20
SMALL = pl.CostEstimate(flops=1, bytes_accessed=1, transcendentals=0)

NT = (((1,), (1,)), ((), ()))
TN = (((0,), (0,)), ((), ()))


def split3(x):
    high = x.astype(jnp.bfloat16)
    rest = x - high.astype(jnp.float32)
    middle = rest.astype(jnp.bfloat16)
    low = (rest - middle.astype(jnp.float32)).astype(jnp.bfloat16)
    return high, middle, low


def state_kernel(heads, key_hbm, value_hbm, decay_hbm, cum_ref, states_ref, reached_ref, end_ref, mid_ref, keys, values, decays, running, sems):
    tokens, width = keys.shape
    dim = width // heads
    size = heads * dim
    blocks = tokens // BLOCK
    decay_copy = pltpu.make_async_copy(decay_hbm, decays, sems.at[2 * blocks])
    decay_copy.start()
    copies = []
    for blk in range(blocks):
        rows = pl.ds(blk * BLOCK, BLOCK)
        copies.append(
            (
                pltpu.make_async_copy(key_hbm.at[rows], keys.at[rows], sems.at[2 * blk]),
                pltpu.make_async_copy(value_hbm.at[rows], values.at[rows], sems.at[2 * blk + 1]),
            )
        )
        copies[-1][0].start()
        copies[-1][1].start()
    upper = jnp.where(
        lax.broadcasted_iota(jnp.int32, (BLOCK, BLOCK), 0) <= lax.broadcasted_iota(jnp.int32, (BLOCK, BLOCK), 1), 1.0, 0.0
    ).astype(jnp.bfloat16)
    decay_copy.wait()
    parts = [
        part for blk in range(blocks) for part in split3(decays[:, blk * BLOCK : (blk + 1) * BLOCK] * LOG2E)
    ]
    sums = jnp.dot(jnp.concatenate(parts, axis=0), upper, preferred_element_type=jnp.float32)
    to_last, decay = [], []
    reached = jnp.zeros((heads, dim), jnp.float32)
    for blk in range(blocks):
        base = 3 * heads * blk
        cum = sums[base : base + heads] + sums[base + heads : base + 2 * heads] + sums[base + 2 * heads : base + 3 * heads]
        cum_ref[:, blk * BLOCK : (blk + 1) * BLOCK] = cum
        last = cum[:, BLOCK - 1 :]
        to_last.append(jnp.exp2(last - cum))
        wide = jnp.broadcast_to(last, (heads, dim))
        decay.append(jnp.exp2(wide))
        reached = reached + wide
        reached_ref[blk] = reached
        if blk == PAGE // BLOCK - 1:
            end_ref[size + 3 * heads :] = jnp.concatenate(split3(reached), axis=0)
    end_ref[size : size + 3 * heads] = jnp.concatenate(split3(reached), axis=0)
    for blk in range(blocks):
        copies[blk][0].wait()
        copies[blk][1].wait()
        here = slice(blk * BLOCK, (blk + 1) * BLOCK)
        for pair in range(heads // 2):
            scaled = []
            for head in (2 * pair, 2 * pair + 1):
                turned = keys[here, head * dim : (head + 1) * dim].T.astype(jnp.float32)
                scaled.append((turned * to_last[blk][head : head + 1]).astype(jnp.bfloat16))
            update = jnp.dot(
                jnp.concatenate(scaled, axis=0),
                values[here, 2 * pair * dim : 2 * (pair + 1) * dim],
                preferred_element_type=jnp.float32,
            )
            for which, head in enumerate((2 * pair, 2 * pair + 1)):
                rows = slice(head * dim, (head + 1) * dim)
                cols = slice(which * dim, (which + 1) * dim)
                state = update[cols, cols]
                if blk:
                    state = state + decay[blk][head : head + 1] * running[rows]
                running[rows] = state
                states_ref[blk, rows] = state.astype(jnp.bfloat16)
                if blk == PAGE // BLOCK - 1:
                    mid_ref[rows] = state.astype(jnp.bfloat16)
                if blk == blocks - 1:
                    end_ref[rows] = state.astype(jnp.bfloat16)


def in_hbm(value):
    return pltpu.with_memory_space_constraint(value, pltpu.HBM)


HBM = pl.BlockSpec(memory_space=pltpu.HBM)
VMEM = pl.BlockSpec(memory_space=pltpu.VMEM)
SMEM = pl.BlockSpec(memory_space=pltpu.SMEM)


def run_states(key_rows, value_rows, decay_log):
    tokens, width = key_rows.shape
    heads = decay_log.shape[0]
    dim = width // heads
    blocks = tokens // BLOCK
    size = heads * dim
    return pl.pallas_call(
        functools.partial(state_kernel, heads),
        in_specs=[HBM] * 3,
        out_specs=[VMEM] * 7,
        out_shape=[
            pltpu.VMEM((heads, tokens), jnp.float32),
            pltpu.VMEM((blocks, size, dim), jnp.bfloat16),
            pltpu.VMEM((blocks, heads, dim), jnp.float32),
            pltpu.VMEM((size + 6 * heads, dim), jnp.bfloat16),
            pltpu.VMEM((size, dim), jnp.bfloat16),
            pltpu.VMEM((tokens, width), jnp.bfloat16),
            pltpu.VMEM((tokens, width), jnp.bfloat16),
        ],
        scratch_shapes=[
            pltpu.VMEM((heads, tokens), jnp.float32),
            pltpu.VMEM((size, dim), jnp.float32),
            pltpu.SemaphoreType.DMA((2 * blocks + 1,)),
        ],
        compiler_params=pltpu.CompilerParams(vmem_limit_bytes=8 * MIB),
        cost_estimate=SMALL,
        name="states",
    )(in_hbm(key_rows), in_hbm(value_rows), in_hbm(decay_log))


def pair_of(one, two):
    zero = jnp.zeros_like(one)
    return jnp.concatenate([jnp.concatenate([one, zero], axis=1), jnp.concatenate([zero, two], axis=1)], axis=0)


def inner_kernel(heads, keys, values, queries, cum_ref, states_ref, reached_ref, out_ref, growth_ref, done_ref):
    step = pl.program_id(0)
    width = queries.shape[1]
    dim = width // heads
    causal = lax.broadcasted_iota(jnp.int32, (BLOCK, BLOCK), 0) >= lax.broadcasted_iota(jnp.int32, (BLOCK, BLOCK), 1)
    blks = [step * (ROWS // BLOCK) + part for part in range(ROWS // BLOCK)]
    here = [pl.ds(pl.multiple_of(blk * BLOCK, BLOCK), BLOCK) for blk in blks]
    before = [jnp.maximum(blk, 1) - 1 for blk in blks]
    cums = [cum_ref[:, rows] for rows in here]
    cum_cols = [cum.T for cum in cums]
    reached = [jnp.where(blk > 0, reached_ref[last], 0.0) for blk, last in zip(blks, before)]
    items = [(head, part) for head in range(heads) for part in range(len(blks))]

    def scores_of(head, part):
        lanes = slice(head * dim, (head + 1) * dim)
        return lax.dot_general(queries[here[part], lanes], keys[here[part], lanes], NT, preferred_element_type=jnp.float32)

    def carried_of(pair, part):
        states = []
        for head in (2 * pair, 2 * pair + 1):
            state = states_ref[before[part], head * dim : (head + 1) * dim]
            states.append(jnp.where(blks[part] > 0, state, jnp.zeros_like(state)))
        query = queries[here[part], 2 * pair * dim : 2 * (pair + 1) * dim]
        return jnp.dot(query, pair_of(*states), preferred_element_type=jnp.float32)

    scores = scores_of(*items[0])
    carried = {}
    for number, (head, part) in enumerate(items):
        ahead = scores_of(*items[number + 1]) if number + 1 < len(items) else None
        if head % 2 == 0:
            carried[part] = carried_of(head // 2, part)
        lanes = slice(head * dim, (head + 1) * dim)
        column = jnp.broadcast_to(cum_cols[part][:, head : head + 1], (BLOCK, dim))
        columns = jnp.concatenate([column] * (BLOCK // dim), axis=1)
        weights = jnp.where(causal, scores * jnp.exp2(columns - cums[part][head : head + 1]), 0.0)
        local = jnp.dot(weights.astype(jnp.bfloat16), values[here[part], lanes], preferred_element_type=jnp.float32)
        which = head % 2
        local = local + carried[part][:, which * dim : (which + 1) * dim] * jnp.exp2(column)
        out_ref[here[part], lanes] = local
        growth_ref[here[part], lanes] = jnp.exp2(column + reached[part][head : head + 1])
        scores = ahead
    done_ref[...] = cums[0][:, :128]


def run_inner(keys, values, queries, cumulative, states, reached):
    tokens, width = keys.shape
    heads = cumulative.shape[0]
    made = pltpu.VMEM((tokens, width), jnp.float32)
    return pl.pallas_call(
        functools.partial(inner_kernel, heads),
        grid=(tokens // ROWS,),
        in_specs=[VMEM] * 6,
        out_specs=[VMEM] * 3,
        out_shape=[made, made, pltpu.VMEM((heads, 128), jnp.float32)],
        compiler_params=pltpu.CompilerParams(vmem_limit_bytes=8 * MIB),
        cost_estimate=SMALL,
        name="inner",
    )(keys, values, queries, cumulative, states, reached)


def read_logs(ends, size, heads):
    whole, first = [], []
    for end in ends:
        parts = end[size:].astype(jnp.float32)
        whole.append(parts[:heads] + parts[heads : 2 * heads] + parts[2 * heads : 3 * heads])
        first.append(parts[3 * heads : 4 * heads] + parts[4 * heads : 5 * heads] + parts[5 * heads :])
    return whole, first


def gather_states(total, ends, places, logs, place, extra, heads, dim):
    factors = []
    for source in range(len(ends)):
        log = extra
        for other, other_log in enumerate(logs):
            between = (places[other] > places[source]) & (places[other] < place)
            log = log + jnp.where(between, other_log, 0.0)
        factors.append(jnp.where(places[source] < place, jnp.exp2(log), 0.0))
    for head in range(heads):
        rows = slice(head * dim, (head + 1) * dim)
        value = jnp.zeros((dim, dim), jnp.float32)
        for source, end in enumerate(ends):
            value += factors[source][head : head + 1] * end[rows].astype(jnp.float32)
        total[rows] = value


def with_entry(heads, here, inner_ref, growth_ref, queries, entry, use):
    dim = entry.shape[1]
    for pair in range(heads // 2):
        rows = [slice(head * dim, (head + 1) * dim) for head in (2 * pair, 2 * pair + 1)]
        carried = jnp.dot(
            queries[here, 2 * pair * dim : 2 * (pair + 1) * dim],
            pair_of(entry[rows[0]], entry[rows[1]]),
            preferred_element_type=jnp.float32,
        )
        for which, lanes in enumerate(rows):
            part = carried[:, which * dim : (which + 1) * dim]
            use(2 * pair + which, inner_ref[here, lanes] + part * growth_ref[here, lanes])


def finish_kernel(heads, inner_ref, growth_ref, queries, *refs):
    *ends, square_ref, entry_ref, entry = refs
    blk = pl.program_id(0)
    tokens, width = queries.shape
    dim = width // heads
    size = heads * dim

    @pl.when(blk == 0)
    def _():
        place = lax.axis_index("seq")
        logs, _unused = read_logs(ends, size, heads)
        places = [place ^ offset for offset in range(len(ends))]
        gather_states(entry, ends, places, logs, place, jnp.zeros((heads, dim), jnp.float32), heads, dim)
        entry_ref[...] = entry[...].astype(jnp.bfloat16)

    total = [jnp.zeros((ROWS, dim), jnp.float32)]

    def use(head, out):
        total[0] = total[0] + out * out

    here = pl.ds(pl.multiple_of(blk * ROWS, ROWS), ROWS)
    with_entry(heads, here, inner_ref, growth_ref, queries, entry_ref, use)
    high = total[0].astype(jnp.bfloat16)
    low = (total[0] - high.astype(jnp.float32)).astype(jnp.bfloat16)
    ones = jnp.ones((8, dim), jnp.bfloat16)
    sums = lax.dot_general(ones, high, NT, preferred_element_type=jnp.float32)
    sums = sums + lax.dot_general(ones, low, NT, preferred_element_type=jnp.float32)
    for row in range(ROWS // 128):
        square_ref[pl.ds(blk * (ROWS // 128) + row, 1)] = sums[:1, row * 128 : (row + 1) * 128]


def run_finish(inner, growth, queries, ends, heads):
    tokens, width = queries.shape
    dim = width // heads
    size = heads * dim
    return pl.pallas_call(
        functools.partial(finish_kernel, heads),
        grid=(tokens // ROWS,),
        in_specs=[VMEM] * (3 + len(ends)),
        out_specs=[VMEM, VMEM],
        out_shape=[pltpu.VMEM((tokens // 128, 128), jnp.float32), pltpu.VMEM((size, dim), jnp.bfloat16)],
        scratch_shapes=[pltpu.VMEM((size, dim), jnp.float32)],
        compiler_params=pltpu.CompilerParams(vmem_limit_bytes=8 * MIB),
        cost_estimate=SMALL,
        name="finish",
    )(inner, growth, queries, *ends)


def scale_kernel(heads, whole_width, inner_ref, growth_ref, queries, entry, gain_ref, square, attended_hbm, made, sems):
    blk = pl.program_id(0)
    tokens, width = made.shape
    dim = width // heads

    def copy_of(part):
        rows = pl.ds(part * ROWS, ROWS)
        return pltpu.make_async_copy(made.at[rows], attended_hbm.at[rows], sems.at[part])

    scales = []
    for part in range(ROWS // 128):
        total = square[pl.ds(blk * (ROWS // 128) + part, 1)]
        scale = lax.rsqrt(total * (1.0 / whole_width) + 1e-06)
        scales.append(jnp.broadcast_to(jnp.broadcast_to(scale, (8, 128)).T[:, :1], (128, dim)))
    scale = jnp.concatenate(scales, axis=0)
    here = pl.ds(pl.multiple_of(blk * ROWS, ROWS), ROWS)

    def use(head, out):
        lanes = slice(head * dim, (head + 1) * dim)
        made[here, lanes] = (out * scale * gain_ref[:, lanes]).astype(jnp.bfloat16)

    with_entry(heads, here, inner_ref, growth_ref, queries, entry, use)
    for part in range(tokens // ROWS):

        @pl.when(blk == part)
        def _():
            copy_of(part).start()

    @pl.when(blk == pl.num_programs(0) - 1)
    def _():
        for part in range(tokens // ROWS):
            copy_of(part).wait()


def run_scale(inner, growth, queries, entry, gain, square, whole_width, heads):
    tokens, width = inner.shape
    return pl.pallas_call(
        functools.partial(scale_kernel, heads, whole_width),
        grid=(tokens // ROWS,),
        in_specs=[VMEM] * 6,
        out_specs=HBM,
        out_shape=jax.ShapeDtypeStruct((tokens, width), jnp.bfloat16),
        scratch_shapes=[pltpu.VMEM((tokens, width), jnp.bfloat16), pltpu.SemaphoreType.DMA((tokens // ROWS,))],
        compiler_params=pltpu.CompilerParams(vmem_limit_bytes=12 * MIB),
        cost_estimate=SMALL,
        name="scale",
    )(inner, growth, queries, entry, gain.reshape(1, width), square)


def own_pages(owner_ref, place, page_of):
    for slot in range(SLOTS):
        page_of[slot] = -1

    def look(page, found):
        mine = (owner_ref[page] == place) & (found < SLOTS)

        @pl.when(mine)
        def _():
            page_of[found] = page

        return found + mine.astype(jnp.int32)

    lax.fori_loop(0, owner_ref.shape[0], look, jnp.int32(0))


def reach_kernel(heads, first, owner_ref, *refs):
    *ends, total, logs_ref, first_ref, page_of = refs
    count = len(ends)
    size, dim = total.shape[1:]
    place = lax.axis_index("seq")
    places = [place ^ offset for offset in range(count)]
    whole, half = read_logs(ends, size, heads)
    for source in range(count):
        logs_ref[source] = whole[source]
        first_ref[source] = half[source]
    own_pages(owner_ref, place, page_of)

    def fill(slot, carry):
        page = page_of[slot + first]

        @pl.when(page >= 0)
        def _():
            until = page // 2 + page % 2
            logs = [logs_ref[source] for source in range(count)]
            extra = jnp.zeros((heads, dim), jnp.float32)
            for source in range(count):
                extra = extra + jnp.where((places[source] == until) & (page % 2 == 0), first_ref[source], 0.0)
            gather_states(total.at[slot], ends, places, logs, until, extra, heads, dim)

        @pl.when(page < 0)
        def _():
            total[slot] = jnp.zeros((size, dim), jnp.float32)

        return carry

    lax.fori_loop(0, total.shape[0], fill, 0)


def run_reach(page_owner, ends, heads, first, slots):
    count = len(ends)
    rows, dim = ends[0].shape
    size = rows - 6 * heads
    return pl.pallas_call(
        functools.partial(reach_kernel, heads, first),
        in_specs=[SMEM] + [VMEM] * count,
        out_specs=VMEM,
        out_shape=pltpu.VMEM((slots, size, dim), jnp.float32),
        scratch_shapes=[
            pltpu.VMEM((count, heads, dim), jnp.float32),
            pltpu.VMEM((count, heads, dim), jnp.float32),
            pltpu.SMEM((SLOTS,), jnp.int32),
        ],
        compiler_params=pltpu.CompilerParams(vmem_limit_bytes=8 * MIB),
        cost_estimate=SMALL,
        name="reach",
    )(page_owner, *ends)


def cache_kernel(count, owner_ref, *refs):
    mids, totals = refs[:count], refs[count:-4]
    cache_hbm, made, page_of, sems = refs[-4:]
    place = lax.axis_index("seq")
    places = [place ^ offset for offset in range(count)]
    own_pages(owner_ref, place, page_of)
    parts = [(total, slot) for total in totals for slot in range(total.shape[0])]
    copies = []
    for slot, (total, row) in enumerate(parts):
        page = page_of[slot]
        halfway = (page >= 0) & (page % 2 == 0)

        @pl.when(jnp.logical_not(halfway))
        def _():
            made[slot] = total[row].astype(jnp.bfloat16)

        for source in range(count):

            @pl.when(halfway & (places[source] == page // 2))
            def _():
                made[slot] = (total[row] + mids[source][...].astype(jnp.float32)).astype(jnp.bfloat16)

        copies.append(pltpu.make_async_copy(made.at[slot], cache_hbm.at[slot], sems.at[slot]))
        copies[-1].start()
    for copy in copies:
        copy.wait()


def run_cache(page_owner, mids, totals):
    size, dim = mids[0].shape
    count = len(mids)
    return pl.pallas_call(
        functools.partial(cache_kernel, count),
        in_specs=[SMEM] + [VMEM] * (count + len(totals)),
        out_specs=HBM,
        out_shape=jax.ShapeDtypeStruct((SLOTS, size, dim), jnp.bfloat16),
        scratch_shapes=[
            pltpu.VMEM((SLOTS, size, dim), jnp.bfloat16),
            pltpu.SMEM((SLOTS,), jnp.int32),
            pltpu.SemaphoreType.DMA((SLOTS,)),
        ],
        compiler_params=pltpu.CompilerParams(vmem_limit_bytes=8 * MIB),
        cost_estimate=SMALL,
        name="cache",
    )(page_owner, *mids, *totals)


def swap(value, axis, offset):
    return lax.ppermute(value, axis, [(place, place ^ offset) for place in range(lax.axis_size(axis))])


def tie(value, *after):
    return lax.optimization_barrier((value, *after))[0]


def add_kernel(one_ref, two_ref, sum_ref):
    sum_ref[...] = one_ref[...] + two_ref[...]


def add(one, two):
    return pl.pallas_call(
        add_kernel,
        in_specs=[VMEM, VMEM],
        out_specs=VMEM,
        out_shape=pltpu.VMEM(one.shape, one.dtype),
        compiler_params=pltpu.CompilerParams(vmem_limit_bytes=4 * MIB),
        cost_estimate=SMALL,
        name="add",
    )(one, two)


def shards(queries, key_rows, value_rows, decay_log, norm_gain, page_owner):
    tokens, width = queries.shape
    heads = decay_log.shape[0]
    dim = width // heads
    count = lax.axis_size("seq")
    cumulative, states, reached, end, mid, keys, values = run_states(key_rows, value_rows, decay_log)
    held = pltpu.with_memory_space_constraint(tie(queries, cumulative), pltpu.VMEM)
    ends, mids = {0: end}, {0: mid}
    for offset in range(2, count, 2):
        ends[offset] = swap(end, "seq", offset)
    ends[1] = swap(end, "seq", 1)
    mids[1] = swap(mid, "seq", 1)
    inner, growth, done = run_inner(keys, values, held, cumulative, states, reached)
    mid = tie(mid, done, ends[1], mids[1])
    for offset in range(2, count, 2):
        mids[offset] = swap(mid, "seq", offset)
    for offset in range(2, count, 2):
        ends[offset + 1] = swap(tie(ends[offset], done), "seq", 1)
    ends = [ends[offset] for offset in range(count)]
    square, entry = run_finish(inner, growth, held, ends, heads)
    totals = []
    shares = [(0, 3), (3, SLOTS - 3)]
    offset = 1
    while offset < lax.axis_size("head"):
        other = swap(square, "head", offset)
        if shares:
            totals.append(run_reach(tie(page_owner, square), ends, heads, *shares.pop(0)))
            other = tie(other, totals[-1])
        square = add(square, other)
        offset *= 2
    for first, slots in shares:
        totals.append(run_reach(tie(page_owner, square), ends, heads, first, slots))
    for offset in range(2, count, 2):
        mids[offset + 1] = swap(tie(mids[offset], square), "seq", 1)
    mids = [mids[offset] for offset in range(count)]
    attended = run_scale(inner, growth, held, entry, norm_gain, square, width * lax.axis_size("head"), heads)
    page_cache = run_cache(page_owner, mids, totals)
    return attended, page_cache.reshape(SLOTS, heads, dim, dim)


def solution(mesh):
    return jax.shard_map(
        shards,
        mesh=mesh,
        in_specs=(
            P("seq", "head"),
            P("seq", "head"),
            P("seq", "head"),
            P("head", "seq"),
            P("head"),
            P(),
        ),
        out_specs=(P("seq", "head"), P("seq", "head", None, None)),
        check_vma=False,
    )
```

```python
import functools
import math

import jax
import jax.numpy as jnp
from jax import lax
from jax.experimental import pallas as pl
from jax.experimental.pallas import tpu as pltpu
from jax.sharding import PartitionSpec as P

BLOCK = 256
ROWS = 512
PAGE = 1024
SLOTS = 5
LOG2E = math.log2(math.e)
MIB = 1 << 20
SMALL = pl.CostEstimate(flops=1, bytes_accessed=1, transcendentals=0)

NT = (((1,), (1,)), ((), ()))
TN = (((0,), (0,)), ((), ()))


def split3(x):
    high = x.astype(jnp.bfloat16)
    rest = x - high.astype(jnp.float32)
    middle = rest.astype(jnp.bfloat16)
    low = (rest - middle.astype(jnp.float32)).astype(jnp.bfloat16)
    return high, middle, low


def state_kernel(heads, key_hbm, value_hbm, decay_hbm, cum_ref, states_ref, reached_ref, end_ref, mid_ref, keys, values, decays, running, sems):
    tokens, width = keys.shape
    dim = width // heads
    size = heads * dim
    blocks = tokens // BLOCK
    decay_copy = pltpu.make_async_copy(decay_hbm, decays, sems.at[2 * blocks])
    decay_copy.start()
    copies = []
    for blk in range(blocks):
        rows = pl.ds(blk * BLOCK, BLOCK)
        copies.append(
            (
                pltpu.make_async_copy(key_hbm.at[rows], keys.at[rows], sems.at[2 * blk]),
                pltpu.make_async_copy(value_hbm.at[rows], values.at[rows], sems.at[2 * blk + 1]),
            )
        )
        copies[-1][0].start()
        copies[-1][1].start()
    upper = jnp.where(
        lax.broadcasted_iota(jnp.int32, (BLOCK, BLOCK), 0) <= lax.broadcasted_iota(jnp.int32, (BLOCK, BLOCK), 1), 1.0, 0.0
    ).astype(jnp.bfloat16)
    decay_copy.wait()
    parts = [
        part for blk in range(blocks) for part in split3(decays[:, blk * BLOCK : (blk + 1) * BLOCK] * LOG2E)
    ]
    sums = jnp.dot(jnp.concatenate(parts, axis=0), upper, preferred_element_type=jnp.float32)
    to_last, decay = [], []
    reached = jnp.zeros((heads, dim), jnp.float32)
    for blk in range(blocks):
        base = 3 * heads * blk
        cum = sums[base : base + heads] + sums[base + heads : base + 2 * heads] + sums[base + 2 * heads : base + 3 * heads]
        cum_ref[:, blk * BLOCK : (blk + 1) * BLOCK] = cum
        last = cum[:, BLOCK - 1 :]
        to_last.append(jnp.exp2(last - cum))
        wide = jnp.broadcast_to(last, (heads, dim))
        decay.append(jnp.exp2(wide))
        reached = reached + wide
        reached_ref[blk] = reached
        if blk == PAGE // BLOCK - 1:
            end_ref[size + 3 * heads :] = jnp.concatenate(split3(reached), axis=0)
    end_ref[size : size + 3 * heads] = jnp.concatenate(split3(reached), axis=0)
    for blk in range(blocks):
        copies[blk][0].wait()
        copies[blk][1].wait()
        here = slice(blk * BLOCK, (blk + 1) * BLOCK)
        for pair in range(heads // 2):
            scaled = []
            for head in (2 * pair, 2 * pair + 1):
                turned = keys[here, head * dim : (head + 1) * dim].T.astype(jnp.float32)
                scaled.append((turned * to_last[blk][head : head + 1]).astype(jnp.bfloat16))
            update = jnp.dot(
                jnp.concatenate(scaled, axis=0),
                values[here, 2 * pair * dim : 2 * (pair + 1) * dim],
                preferred_element_type=jnp.float32,
            )
            for which, head in enumerate((2 * pair, 2 * pair + 1)):
                rows = slice(head * dim, (head + 1) * dim)
                cols = slice(which * dim, (which + 1) * dim)
                state = update[cols, cols]
                if blk:
                    state = state + decay[blk][head : head + 1] * running[rows]
                running[rows] = state
                states_ref[blk, rows] = state.astype(jnp.bfloat16)
                if blk == PAGE // BLOCK - 1:
                    mid_ref[rows] = state.astype(jnp.bfloat16)
                if blk == blocks - 1:
                    end_ref[rows] = state.astype(jnp.bfloat16)


def in_hbm(value):
    return pltpu.with_memory_space_constraint(value, pltpu.HBM)


HBM = pl.BlockSpec(memory_space=pltpu.HBM)
VMEM = pl.BlockSpec(memory_space=pltpu.VMEM)
SMEM = pl.BlockSpec(memory_space=pltpu.SMEM)


def run_states(key_rows, value_rows, decay_log):
    tokens, width = key_rows.shape
    heads = decay_log.shape[0]
    dim = width // heads
    blocks = tokens // BLOCK
    size = heads * dim
    return pl.pallas_call(
        functools.partial(state_kernel, heads),
        in_specs=[HBM] * 3,
        out_specs=[VMEM] * 7,
        out_shape=[
            pltpu.VMEM((heads, tokens), jnp.float32),
            pltpu.VMEM((blocks, size, dim), jnp.bfloat16),
            pltpu.VMEM((blocks, heads, dim), jnp.float32),
            pltpu.VMEM((size + 6 * heads, dim), jnp.bfloat16),
            pltpu.VMEM((size, dim), jnp.bfloat16),
            pltpu.VMEM((tokens, width), jnp.bfloat16),
            pltpu.VMEM((tokens, width), jnp.bfloat16),
        ],
        scratch_shapes=[
            pltpu.VMEM((heads, tokens), jnp.float32),
            pltpu.VMEM((size, dim), jnp.float32),
            pltpu.SemaphoreType.DMA((2 * blocks + 1,)),
        ],
        compiler_params=pltpu.CompilerParams(vmem_limit_bytes=8 * MIB),
        cost_estimate=SMALL,
        name="states",
    )(in_hbm(key_rows), in_hbm(value_rows), in_hbm(decay_log))


def pair_of(one, two):
    zero = jnp.zeros_like(one)
    return jnp.concatenate([jnp.concatenate([one, zero], axis=1), jnp.concatenate([zero, two], axis=1)], axis=0)


def inner_kernel(heads, keys, values, queries, cum_ref, states_ref, reached_ref, out_ref, grown_ref, done_ref):
    step = pl.program_id(0)
    width = queries.shape[1]
    dim = width // heads
    causal = lax.broadcasted_iota(jnp.int32, (BLOCK, BLOCK), 0) >= lax.broadcasted_iota(jnp.int32, (BLOCK, BLOCK), 1)
    blks = [step * (ROWS // BLOCK) + part for part in range(ROWS // BLOCK)]
    here = [pl.ds(pl.multiple_of(blk * BLOCK, BLOCK), BLOCK) for blk in blks]
    before = [jnp.maximum(blk, 1) - 1 for blk in blks]
    cums = [cum_ref[:, rows] for rows in here]
    cum_cols = [cum.T for cum in cums]
    reached = [jnp.where(blk > 0, reached_ref[last], 0.0) for blk, last in zip(blks, before)]
    items = [(head, part) for head in range(heads) for part in range(len(blks))]

    def scores_of(head, part):
        lanes = slice(head * dim, (head + 1) * dim)
        return lax.dot_general(queries[here[part], lanes], keys[here[part], lanes], NT, preferred_element_type=jnp.float32)

    def carried_of(pair, part):
        states = []
        for head in (2 * pair, 2 * pair + 1):
            state = states_ref[before[part], head * dim : (head + 1) * dim]
            states.append(jnp.where(blks[part] > 0, state, jnp.zeros_like(state)))
        query = queries[here[part], 2 * pair * dim : 2 * (pair + 1) * dim]
        return jnp.dot(query, pair_of(*states), preferred_element_type=jnp.float32)

    scores = scores_of(*items[0])
    carried = {}
    for number, (head, part) in enumerate(items):
        ahead = scores_of(*items[number + 1]) if number + 1 < len(items) else None
        if head % 2 == 0:
            carried[part] = carried_of(head // 2, part)
        lanes = slice(head * dim, (head + 1) * dim)
        column = jnp.broadcast_to(cum_cols[part][:, head : head + 1], (BLOCK, dim))
        columns = jnp.concatenate([column] * (BLOCK // dim), axis=1)
        weights = jnp.where(causal, scores * jnp.exp2(columns - cums[part][head : head + 1]), 0.0)
        local = jnp.dot(weights.astype(jnp.bfloat16), values[here[part], lanes], preferred_element_type=jnp.float32)
        which = head % 2
        local = local + carried[part][:, which * dim : (which + 1) * dim] * jnp.exp2(column)
        out_ref[here[part], lanes] = local
        growth = jnp.exp2(column + reached[part][head : head + 1])
        grown_ref[here[part], lanes] = (queries[here[part], lanes].astype(jnp.float32) * growth).astype(jnp.bfloat16)
        scores = ahead
    done_ref[...] = cums[0][:, :128]


def run_inner(keys, values, queries, cumulative, states, reached):
    tokens, width = keys.shape
    heads = cumulative.shape[0]
    made = pltpu.VMEM((tokens, width), jnp.float32)
    return pl.pallas_call(
        functools.partial(inner_kernel, heads),
        grid=(tokens // ROWS,),
        in_specs=[VMEM] * 6,
        out_specs=[VMEM] * 3,
        out_shape=[made, pltpu.VMEM((tokens, width), jnp.bfloat16), pltpu.VMEM((heads, 128), jnp.float32)],
        compiler_params=pltpu.CompilerParams(vmem_limit_bytes=8 * MIB),
        cost_estimate=SMALL,
        name="inner",
    )(keys, values, queries, cumulative, states, reached)


def read_logs(ends, size, heads):
    whole, first = [], []
    for end in ends:
        parts = end[size:].astype(jnp.float32)
        whole.append(parts[:heads] + parts[heads : 2 * heads] + parts[2 * heads : 3 * heads])
        first.append(parts[3 * heads : 4 * heads] + parts[4 * heads : 5 * heads] + parts[5 * heads :])
    return whole, first


def gather_states(total, ends, places, logs, place, extra, heads, dim):
    factors = []
    for source in range(len(ends)):
        log = extra
        for other, other_log in enumerate(logs):
            between = (places[other] > places[source]) & (places[other] < place)
            log = log + jnp.where(between, other_log, 0.0)
        factors.append(jnp.where(places[source] < place, jnp.exp2(log), 0.0))
    for head in range(heads):
        rows = slice(head * dim, (head + 1) * dim)
        value = jnp.zeros((dim, dim), jnp.float32)
        for source, end in enumerate(ends):
            value += factors[source][head : head + 1] * end[rows].astype(jnp.float32)
        total[rows] = value


def finish_kernel(heads, inner_ref, grown, gain_ref, *refs):
    *ends, out_ref, square_ref, entry, entry_low = refs
    blk = pl.program_id(0)
    width = grown.shape[1]
    dim = width // heads
    size = heads * dim

    @pl.when(blk == 0)
    def _():
        place = lax.axis_index("seq")
        logs, _unused = read_logs(ends, size, heads)
        places = [place ^ offset for offset in range(len(ends))]
        gather_states(entry, ends, places, logs, place, jnp.zeros((heads, dim), jnp.float32), heads, dim)
        entry_low[...] = entry[...].astype(jnp.bfloat16)

    here = pl.ds(pl.multiple_of(blk * ROWS, ROWS), ROWS)

    def carried_of(pair):
        rows = [slice(head * dim, (head + 1) * dim) for head in (2 * pair, 2 * pair + 1)]
        query = grown[here, 2 * pair * dim : 2 * (pair + 1) * dim]
        return jnp.dot(query, pair_of(entry_low[rows[0]], entry_low[rows[1]]), preferred_element_type=jnp.float32)

    total = jnp.zeros((ROWS, dim), jnp.float32)
    ahead = carried_of(0)
    for pair in range(heads // 2):
        carried = ahead
        if pair + 1 < heads // 2:
            ahead = carried_of(pair + 1)
        for which in range(2):
            lanes = slice((2 * pair + which) * dim, (2 * pair + which + 1) * dim)
            out = inner_ref[here, lanes] + carried[:, which * dim : (which + 1) * dim]
            total += out * out
            out_ref[here, lanes] = out * gain_ref[:, lanes]
    high = total.astype(jnp.bfloat16)
    low = (total - high.astype(jnp.float32)).astype(jnp.bfloat16)
    ones = jnp.ones((8, dim), jnp.bfloat16)
    sums = lax.dot_general(ones, high, NT, preferred_element_type=jnp.float32)
    sums = sums + lax.dot_general(ones, low, NT, preferred_element_type=jnp.float32)
    for row in range(ROWS // 128):
        square_ref[pl.ds(blk * (ROWS // 128) + row, 1)] = sums[:1, row * 128 : (row + 1) * 128]


def run_finish(inner, grown, gain, ends, heads):
    tokens, width = grown.shape
    dim = width // heads
    size = heads * dim
    return pl.pallas_call(
        functools.partial(finish_kernel, heads),
        grid=(tokens // ROWS,),
        in_specs=[VMEM] * (3 + len(ends)),
        out_specs=[VMEM, VMEM],
        out_shape=[pltpu.VMEM((tokens, width), jnp.float32), pltpu.VMEM((tokens // 128, 128), jnp.float32)],
        scratch_shapes=[pltpu.VMEM((size, dim), jnp.float32), pltpu.VMEM((size, dim), jnp.bfloat16)],
        compiler_params=pltpu.CompilerParams(vmem_limit_bytes=8 * MIB),
        cost_estimate=SMALL,
        name="finish",
    )(inner, grown, gain.reshape(1, width), *ends)


def scale_kernel(whole_width, out_ref, square, attended_hbm, made, sems):
    blk = pl.program_id(0)
    tokens, width = made.shape

    def copy_of(part):
        rows = pl.ds(part * BLOCK, BLOCK)
        return pltpu.make_async_copy(made.at[rows], attended_hbm.at[rows], sems.at[part])

    for sub in range(ROWS // BLOCK):
        base = blk * ROWS + sub * BLOCK
        scales = []
        for part in range(BLOCK // 128):
            total = square[pl.ds(blk * (ROWS // 128) + sub * (BLOCK // 128) + part, 1)]
            scale = lax.rsqrt(total * (1.0 / whole_width) + 1e-06)
            scales.append(jnp.broadcast_to(jnp.broadcast_to(scale, (8, 128)).T[:, :1], (128, 128)))
        scale = jnp.concatenate(scales, axis=0)
        here = pl.ds(pl.multiple_of(base, BLOCK), BLOCK)
        for col in range(0, width, 128):
            made[here, col : col + 128] = (out_ref[here, col : col + 128] * scale).astype(jnp.bfloat16)
        for step in range(tokens // ROWS):

            @pl.when(blk == step)
            def _():
                copy_of(step * (ROWS // BLOCK) + sub).start()

    @pl.when(blk == pl.num_programs(0) - 1)
    def _():
        for part in range(tokens // BLOCK):
            copy_of(part).wait()


def run_scale(out, square, whole_width):
    tokens, width = out.shape
    return pl.pallas_call(
        functools.partial(scale_kernel, whole_width),
        grid=(tokens // ROWS,),
        in_specs=[VMEM] * 2,
        out_specs=HBM,
        out_shape=jax.ShapeDtypeStruct((tokens, width), jnp.bfloat16),
        scratch_shapes=[pltpu.VMEM((tokens, width), jnp.bfloat16), pltpu.SemaphoreType.DMA((tokens // BLOCK,))],
        compiler_params=pltpu.CompilerParams(vmem_limit_bytes=12 * MIB),
        cost_estimate=SMALL,
        name="scale",
    )(out, square)


def own_pages(owner_ref, place, page_of):
    for slot in range(SLOTS):
        page_of[slot] = -1

    def look(page, found):
        mine = (owner_ref[page] == place) & (found < SLOTS)

        @pl.when(mine)
        def _():
            page_of[found] = page

        return found + mine.astype(jnp.int32)

    lax.fori_loop(0, owner_ref.shape[0], look, jnp.int32(0))


def reach_kernel(heads, first, owner_ref, *refs):
    *ends, total, logs_ref, first_ref, page_of = refs
    count = len(ends)
    size, dim = total.shape[1:]
    place = lax.axis_index("seq")
    places = [place ^ offset for offset in range(count)]
    whole, half = read_logs(ends, size, heads)
    for source in range(count):
        logs_ref[source] = whole[source]
        first_ref[source] = half[source]
    own_pages(owner_ref, place, page_of)

    def fill(slot, carry):
        page = page_of[slot + first]

        @pl.when(page >= 0)
        def _():
            until = page // 2 + page % 2
            logs = [logs_ref[source] for source in range(count)]
            extra = jnp.zeros((heads, dim), jnp.float32)
            for source in range(count):
                extra = extra + jnp.where((places[source] == until) & (page % 2 == 0), first_ref[source], 0.0)
            gather_states(total.at[slot], ends, places, logs, until, extra, heads, dim)

        @pl.when(page < 0)
        def _():
            total[slot] = jnp.zeros((size, dim), jnp.float32)

        return carry

    lax.fori_loop(0, total.shape[0], fill, 0)


def run_reach(page_owner, ends, heads, first, slots):
    count = len(ends)
    rows, dim = ends[0].shape
    size = rows - 6 * heads
    return pl.pallas_call(
        functools.partial(reach_kernel, heads, first),
        in_specs=[SMEM] + [VMEM] * count,
        out_specs=VMEM,
        out_shape=pltpu.VMEM((slots, size, dim), jnp.float32),
        scratch_shapes=[
            pltpu.VMEM((count, heads, dim), jnp.float32),
            pltpu.VMEM((count, heads, dim), jnp.float32),
            pltpu.SMEM((SLOTS,), jnp.int32),
        ],
        compiler_params=pltpu.CompilerParams(vmem_limit_bytes=8 * MIB),
        cost_estimate=SMALL,
        name="reach",
    )(page_owner, *ends)


def cache_kernel(count, owner_ref, *refs):
    mids, totals = refs[:count], refs[count:-4]
    cache_hbm, made, page_of, sems = refs[-4:]
    place = lax.axis_index("seq")
    places = [place ^ offset for offset in range(count)]
    own_pages(owner_ref, place, page_of)
    parts = [(total, slot) for total in totals for slot in range(total.shape[0])]
    copies = []
    for slot, (total, row) in enumerate(parts):
        page = page_of[slot]
        halfway = (page >= 0) & (page % 2 == 0)

        @pl.when(jnp.logical_not(halfway))
        def _():
            made[slot] = total[row].astype(jnp.bfloat16)

        for source in range(count):

            @pl.when(halfway & (places[source] == page // 2))
            def _():
                made[slot] = (total[row] + mids[source][...].astype(jnp.float32)).astype(jnp.bfloat16)

        copies.append(pltpu.make_async_copy(made.at[slot], cache_hbm.at[slot], sems.at[slot]))
        copies[-1].start()
    for copy in copies:
        copy.wait()


def run_cache(page_owner, mids, totals):
    size, dim = mids[0].shape
    count = len(mids)
    return pl.pallas_call(
        functools.partial(cache_kernel, count),
        in_specs=[SMEM] + [VMEM] * (count + len(totals)),
        out_specs=HBM,
        out_shape=jax.ShapeDtypeStruct((SLOTS, size, dim), jnp.bfloat16),
        scratch_shapes=[
            pltpu.VMEM((SLOTS, size, dim), jnp.bfloat16),
            pltpu.SMEM((SLOTS,), jnp.int32),
            pltpu.SemaphoreType.DMA((SLOTS,)),
        ],
        compiler_params=pltpu.CompilerParams(vmem_limit_bytes=8 * MIB),
        cost_estimate=SMALL,
        name="cache",
    )(page_owner, *mids, *totals)


def swap(value, axis, offset):
    return lax.ppermute(value, axis, [(place, place ^ offset) for place in range(lax.axis_size(axis))])


def tie(value, *after):
    return lax.optimization_barrier((value, *after))[0]


def add_kernel(one_ref, two_ref, sum_ref):
    sum_ref[...] = one_ref[...] + two_ref[...]


def add(one, two):
    return pl.pallas_call(
        add_kernel,
        in_specs=[VMEM, VMEM],
        out_specs=VMEM,
        out_shape=pltpu.VMEM(one.shape, one.dtype),
        compiler_params=pltpu.CompilerParams(vmem_limit_bytes=4 * MIB),
        cost_estimate=SMALL,
        name="add",
    )(one, two)


def shards(queries, key_rows, value_rows, decay_log, norm_gain, page_owner):
    tokens, width = queries.shape
    heads = decay_log.shape[0]
    dim = width // heads
    count = lax.axis_size("seq")
    cumulative, states, reached, end, mid, keys, values = run_states(key_rows, value_rows, decay_log)
    held = pltpu.with_memory_space_constraint(tie(queries, cumulative), pltpu.VMEM)
    ends, mids = {0: end}, {0: mid}
    for offset in range(2, count, 2):
        ends[offset] = swap(end, "seq", offset)
    ends[1] = swap(end, "seq", 1)
    mids[1] = swap(mid, "seq", 1)
    inner, grown, done = run_inner(keys, values, held, cumulative, states, reached)
    mid = tie(mid, done, ends[1], mids[1])
    for offset in range(2, count, 2):
        mids[offset] = swap(mid, "seq", offset)
    for offset in range(2, count, 2):
        ends[offset + 1] = swap(tie(ends[offset], done), "seq", 1)
    ends = [ends[offset] for offset in range(count)]
    out, square = run_finish(inner, grown, norm_gain, ends, heads)
    totals = []
    shares = [(0, 3), (3, SLOTS - 3)]
    offset = 1
    while offset < lax.axis_size("head"):
        other = swap(square, "head", offset)
        if shares:
            totals.append(run_reach(tie(page_owner, square), ends, heads, *shares.pop(0)))
            other = tie(other, totals[-1])
        square = add(square, other)
        if offset == 1:
            for part in range(2, count, 2):
                if part != count - 2:
                    mids[part + 1] = swap(tie(mids[part], square), "seq", 1)
        offset *= 2
    for first, slots in shares:
        totals.append(run_reach(tie(page_owner, square), ends, heads, first, slots))
    mids[count - 1] = swap(tie(mids[count - 2], square), "seq", 1)
    mids = [mids[offset] for offset in range(count)]
    attended = run_scale(out, square, width * lax.axis_size("head"))
    page_cache = run_cache(page_owner, mids, totals)
    return attended, page_cache.reshape(SLOTS, heads, dim, dim)


def solution(mesh):
    return jax.shard_map(
        shards,
        mesh=mesh,
        in_specs=(
            P("seq", "head"),
            P("seq", "head"),
            P("seq", "head"),
            P("head", "seq"),
            P("head"),
            P(),
        ),
        out_specs=(P("seq", "head"), P("seq", "head", None, None)),
        check_vma=False,
    )
```

```python
import functools
import math

import jax
import jax.numpy as jnp
from jax import lax
from jax.experimental import pallas as pl
from jax.experimental.pallas import tpu as pltpu
from jax.sharding import PartitionSpec as P

BLOCK = 256
ROWS = 512
PAGE = 1024
SLOTS = 5
LOG2E = math.log2(math.e)
MIB = 1 << 20
SMALL = pl.CostEstimate(flops=1, bytes_accessed=1, transcendentals=0)

NT = (((1,), (1,)), ((), ()))
TN = (((0,), (0,)), ((), ()))


def split3(x):
    high = x.astype(jnp.bfloat16)
    rest = x - high.astype(jnp.float32)
    middle = rest.astype(jnp.bfloat16)
    low = (rest - middle.astype(jnp.float32)).astype(jnp.bfloat16)
    return high, middle, low


def state_kernel(heads, key_hbm, value_hbm, decay_hbm, cum_ref, states_ref, reached_ref, end_ref, mid_ref, keys, values, decays, running, sems):
    tokens, width = keys.shape
    dim = width // heads
    size = heads * dim
    blocks = tokens // BLOCK
    decay_copy = pltpu.make_async_copy(decay_hbm, decays, sems.at[2 * blocks])
    decay_copy.start()
    copies = []
    for blk in range(blocks):
        rows = pl.ds(blk * BLOCK, BLOCK)
        copies.append(
            (
                pltpu.make_async_copy(key_hbm.at[rows], keys.at[rows], sems.at[2 * blk]),
                pltpu.make_async_copy(value_hbm.at[rows], values.at[rows], sems.at[2 * blk + 1]),
            )
        )
        copies[-1][0].start()
        copies[-1][1].start()
    upper = jnp.where(
        lax.broadcasted_iota(jnp.int32, (BLOCK, BLOCK), 0) <= lax.broadcasted_iota(jnp.int32, (BLOCK, BLOCK), 1), 1.0, 0.0
    ).astype(jnp.bfloat16)
    decay_copy.wait()
    parts = [
        part for blk in range(blocks) for part in split3(decays[:, blk * BLOCK : (blk + 1) * BLOCK] * LOG2E)
    ]
    sums = jnp.dot(jnp.concatenate(parts, axis=0), upper, preferred_element_type=jnp.float32)
    to_last, decay = [], []
    reached = jnp.zeros((heads, dim), jnp.float32)
    for blk in range(blocks):
        base = 3 * heads * blk
        cum = sums[base : base + heads] + sums[base + heads : base + 2 * heads] + sums[base + 2 * heads : base + 3 * heads]
        cum_ref[:, blk * BLOCK : (blk + 1) * BLOCK] = cum
        last = cum[:, BLOCK - 1 :]
        to_last.append(jnp.exp2(last - cum))
        wide = jnp.broadcast_to(last, (heads, dim))
        decay.append(jnp.exp2(wide))
        reached = reached + wide
        reached_ref[blk] = reached
        if blk == PAGE // BLOCK - 1:
            end_ref[size + 3 * heads :] = jnp.concatenate(split3(reached), axis=0)
    end_ref[size : size + 3 * heads] = jnp.concatenate(split3(reached), axis=0)
    for blk in range(blocks):
        copies[blk][0].wait()
        copies[blk][1].wait()
        here = slice(blk * BLOCK, (blk + 1) * BLOCK)
        for pair in range(heads // 2):
            scaled = []
            for head in (2 * pair, 2 * pair + 1):
                turned = keys[here, head * dim : (head + 1) * dim].T.astype(jnp.float32)
                scaled.append((turned * to_last[blk][head : head + 1]).astype(jnp.bfloat16))
            update = jnp.dot(
                jnp.concatenate(scaled, axis=0),
                values[here, 2 * pair * dim : 2 * (pair + 1) * dim],
                preferred_element_type=jnp.float32,
            )
            for which, head in enumerate((2 * pair, 2 * pair + 1)):
                rows = slice(head * dim, (head + 1) * dim)
                cols = slice(which * dim, (which + 1) * dim)
                state = update[cols, cols]
                if blk:
                    state = state + decay[blk][head : head + 1] * running[rows]
                running[rows] = state
                states_ref[blk, rows] = state.astype(jnp.bfloat16)
                if blk == PAGE // BLOCK - 1:
                    mid_ref[rows] = state.astype(jnp.bfloat16)
                if blk == blocks - 1:
                    end_ref[rows] = state.astype(jnp.bfloat16)


def in_hbm(value):
    return pltpu.with_memory_space_constraint(value, pltpu.HBM)


HBM = pl.BlockSpec(memory_space=pltpu.HBM)
VMEM = pl.BlockSpec(memory_space=pltpu.VMEM)
SMEM = pl.BlockSpec(memory_space=pltpu.SMEM)


def run_states(key_rows, value_rows, decay_log):
    tokens, width = key_rows.shape
    heads = decay_log.shape[0]
    dim = width // heads
    blocks = tokens // BLOCK
    size = heads * dim
    return pl.pallas_call(
        functools.partial(state_kernel, heads),
        in_specs=[HBM] * 3,
        out_specs=[VMEM] * 7,
        out_shape=[
            pltpu.VMEM((heads, tokens), jnp.float32),
            pltpu.VMEM((blocks, size, dim), jnp.bfloat16),
            pltpu.VMEM((blocks, heads, dim), jnp.float32),
            pltpu.VMEM((size + 6 * heads, dim), jnp.bfloat16),
            pltpu.VMEM((size, dim), jnp.bfloat16),
            pltpu.VMEM((tokens, width), jnp.bfloat16),
            pltpu.VMEM((tokens, width), jnp.bfloat16),
        ],
        scratch_shapes=[
            pltpu.VMEM((heads, tokens), jnp.float32),
            pltpu.VMEM((size, dim), jnp.float32),
            pltpu.SemaphoreType.DMA((2 * blocks + 1,)),
        ],
        compiler_params=pltpu.CompilerParams(vmem_limit_bytes=8 * MIB),
        cost_estimate=SMALL,
        name="states",
    )(in_hbm(key_rows), in_hbm(value_rows), in_hbm(decay_log))


def pair_of(one, two):
    zero = jnp.zeros_like(one)
    return jnp.concatenate([jnp.concatenate([one, zero], axis=1), jnp.concatenate([zero, two], axis=1)], axis=0)


def inner_kernel(heads, keys, values, queries, cum_ref, states_ref, reached_ref, out_ref, grown_ref, done_ref):
    step = pl.program_id(0)
    width = queries.shape[1]
    dim = width // heads
    causal = lax.broadcasted_iota(jnp.int32, (BLOCK, BLOCK), 0) >= lax.broadcasted_iota(jnp.int32, (BLOCK, BLOCK), 1)
    blks = [step * (ROWS // BLOCK) + part for part in range(ROWS // BLOCK)]
    here = [pl.ds(pl.multiple_of(blk * BLOCK, BLOCK), BLOCK) for blk in blks]
    before = [jnp.maximum(blk, 1) - 1 for blk in blks]
    cums = [cum_ref[:, rows] for rows in here]
    cum_cols = [cum.T for cum in cums]
    reached = [jnp.where(blk > 0, reached_ref[last], 0.0) for blk, last in zip(blks, before)]
    items = [(pair + which, part) for pair in range(0, heads, 2) for part in range(len(blks)) for which in range(2)]

    def scores_of(head, part):
        lanes = slice(head * dim, (head + 1) * dim)
        return lax.dot_general(queries[here[part], lanes], keys[here[part], lanes], NT, preferred_element_type=jnp.float32)

    def carried_of(pair, part):
        states = []
        for head in (2 * pair, 2 * pair + 1):
            state = states_ref[before[part], head * dim : (head + 1) * dim]
            states.append(jnp.where(blks[part] > 0, state, jnp.zeros_like(state)))
        query = queries[here[part], 2 * pair * dim : 2 * (pair + 1) * dim]
        return jnp.dot(query, pair_of(*states), preferred_element_type=jnp.float32)

    scores = scores_of(*items[0])
    carried = {}
    for number, (head, part) in enumerate(items):
        ahead = scores_of(*items[number + 1]) if number + 1 < len(items) else None
        if head % 2 == 0:
            carried[part] = carried_of(head // 2, part)
        lanes = slice(head * dim, (head + 1) * dim)
        column = jnp.broadcast_to(cum_cols[part][:, head : head + 1], (BLOCK, dim))
        columns = jnp.concatenate([column] * (BLOCK // dim), axis=1)
        weights = jnp.where(causal, scores * jnp.exp2(columns - cums[part][head : head + 1]), 0.0)
        local = jnp.dot(weights.astype(jnp.bfloat16), values[here[part], lanes], preferred_element_type=jnp.float32)
        which = head % 2
        local = local + carried[part][:, which * dim : (which + 1) * dim] * jnp.exp2(column)
        out_ref[here[part], lanes] = local
        growth = jnp.exp2(column + reached[part][head : head + 1])
        grown_ref[here[part], lanes] = (queries[here[part], lanes].astype(jnp.float32) * growth).astype(jnp.bfloat16)
        scores = ahead
    done_ref[...] = cums[0][:, :128]


def run_inner(keys, values, queries, cumulative, states, reached):
    tokens, width = keys.shape
    heads = cumulative.shape[0]
    made = pltpu.VMEM((tokens, width), jnp.float32)
    return pl.pallas_call(
        functools.partial(inner_kernel, heads),
        grid=(tokens // ROWS,),
        in_specs=[VMEM] * 6,
        out_specs=[VMEM] * 3,
        out_shape=[made, pltpu.VMEM((tokens, width), jnp.bfloat16), pltpu.VMEM((heads, 128), jnp.float32)],
        compiler_params=pltpu.CompilerParams(vmem_limit_bytes=8 * MIB),
        cost_estimate=SMALL,
        name="inner",
    )(keys, values, queries, cumulative, states, reached)


def read_logs(ends, size, heads):
    whole, first = [], []
    for end in ends:
        parts = end[size:].astype(jnp.float32)
        whole.append(parts[:heads] + parts[heads : 2 * heads] + parts[2 * heads : 3 * heads])
        first.append(parts[3 * heads : 4 * heads] + parts[4 * heads : 5 * heads] + parts[5 * heads :])
    return whole, first


def gather_states(total, ends, places, logs, place, extra, heads, dim):
    factors = []
    for source in range(len(ends)):
        log = extra
        for other, other_log in enumerate(logs):
            between = (places[other] > places[source]) & (places[other] < place)
            log = log + jnp.where(between, other_log, 0.0)
        factors.append(jnp.where(places[source] < place, jnp.exp2(log), 0.0))
    for head in range(heads):
        rows = slice(head * dim, (head + 1) * dim)
        value = jnp.zeros((dim, dim), jnp.float32)
        for source, end in enumerate(ends):
            value += factors[source][head : head + 1] * end[rows].astype(jnp.float32)
        total[rows] = value


def finish_kernel(heads, inner_ref, grown, gain_ref, *refs):
    *ends, out_ref, square_ref, entry, entry_low = refs
    blk = pl.program_id(0)
    tokens, width = grown.shape
    length = PAGE
    dim = width // heads
    size = heads * dim

    @pl.when(blk == 0)
    def _():
        place = lax.axis_index("seq")
        logs, _unused = read_logs(ends, size, heads)
        places = [place ^ offset for offset in range(len(ends))]
        gather_states(entry, ends, places, logs, place, jnp.zeros((heads, dim), jnp.float32), heads, dim)
        entry_low[...] = entry[...].astype(jnp.bfloat16)

    here = pl.ds(pl.multiple_of(blk * length, length), length)

    def carried_of(pair):
        rows = [slice(head * dim, (head + 1) * dim) for head in (2 * pair, 2 * pair + 1)]
        query = grown[here, 2 * pair * dim : 2 * (pair + 1) * dim]
        return jnp.dot(query, pair_of(entry_low[rows[0]], entry_low[rows[1]]), preferred_element_type=jnp.float32)

    total = jnp.zeros((length, dim), jnp.float32)
    ahead = carried_of(0)
    for pair in range(heads // 2):
        carried = ahead
        if pair + 1 < heads // 2:
            ahead = carried_of(pair + 1)
        lanes = slice(2 * pair * dim, 2 * (pair + 1) * dim)
        out = inner_ref[here, lanes] + carried
        squares = out * out
        total += squares[:, :dim] + squares[:, dim:]
        out_ref[here, lanes] = out * gain_ref[:, lanes]
    high = total.astype(jnp.bfloat16)
    low = (total - high.astype(jnp.float32)).astype(jnp.bfloat16)
    ones = jnp.ones((8, dim), jnp.bfloat16)
    sums = lax.dot_general(ones, high, NT, preferred_element_type=jnp.float32)
    sums = sums + lax.dot_general(ones, low, NT, preferred_element_type=jnp.float32)
    for row in range(length // 128):
        square_ref[pl.ds(blk * (length // 128) + row, 1)] = sums[:1, row * 128 : (row + 1) * 128]


def run_finish(inner, grown, gain, ends, heads):
    tokens, width = grown.shape
    dim = width // heads
    size = heads * dim
    return pl.pallas_call(
        functools.partial(finish_kernel, heads),
        grid=(tokens // PAGE,),
        in_specs=[VMEM] * (3 + len(ends)),
        out_specs=[VMEM, VMEM],
        out_shape=[pltpu.VMEM((tokens, width), jnp.float32), pltpu.VMEM((tokens // 128, 128), jnp.float32)],
        scratch_shapes=[pltpu.VMEM((size, dim), jnp.float32), pltpu.VMEM((size, dim), jnp.bfloat16)],
        compiler_params=pltpu.CompilerParams(vmem_limit_bytes=8 * MIB),
        cost_estimate=SMALL,
        name="finish",
    )(inner, grown, gain.reshape(1, width), *ends)


def scale_kernel(whole_width, out_ref, square, attended_hbm, made, sems):
    blk = pl.program_id(0)
    tokens, width = made.shape

    def copy_of(part):
        rows = pl.ds(part * BLOCK, BLOCK)
        return pltpu.make_async_copy(made.at[rows], attended_hbm.at[rows], sems.at[part])

    for sub in range(ROWS // BLOCK):
        base = blk * ROWS + sub * BLOCK
        scales = []
        for part in range(BLOCK // 128):
            total = square[pl.ds(blk * (ROWS // 128) + sub * (BLOCK // 128) + part, 1)]
            scale = lax.rsqrt(total * (1.0 / whole_width) + 1e-06)
            scales.append(jnp.broadcast_to(jnp.broadcast_to(scale, (8, 128)).T[:, :1], (128, 128)))
        scale = jnp.concatenate(scales, axis=0)
        here = pl.ds(pl.multiple_of(base, BLOCK), BLOCK)
        for col in range(0, width, 128):
            made[here, col : col + 128] = (out_ref[here, col : col + 128] * scale).astype(jnp.bfloat16)
        for step in range(tokens // ROWS):

            @pl.when(blk == step)
            def _():
                copy_of(step * (ROWS // BLOCK) + sub).start()

    @pl.when(blk == pl.num_programs(0) - 1)
    def _():
        for part in range(tokens // BLOCK):
            copy_of(part).wait()


def run_scale(out, square, whole_width):
    tokens, width = out.shape
    return pl.pallas_call(
        functools.partial(scale_kernel, whole_width),
        grid=(tokens // ROWS,),
        in_specs=[VMEM] * 2,
        out_specs=HBM,
        out_shape=jax.ShapeDtypeStruct((tokens, width), jnp.bfloat16),
        scratch_shapes=[pltpu.VMEM((tokens, width), jnp.bfloat16), pltpu.SemaphoreType.DMA((tokens // BLOCK,))],
        compiler_params=pltpu.CompilerParams(vmem_limit_bytes=12 * MIB),
        cost_estimate=SMALL,
        name="scale",
    )(out, square)


def own_pages(owner_ref, place, page_of):
    for slot in range(SLOTS):
        page_of[slot] = -1

    def look(page, found):
        mine = (owner_ref[page] == place) & (found < SLOTS)

        @pl.when(mine)
        def _():
            page_of[found] = page

        return found + mine.astype(jnp.int32)

    lax.fori_loop(0, owner_ref.shape[0], look, jnp.int32(0))


def reach_kernel(heads, first, owner_ref, *refs):
    *ends, total, logs_ref, first_ref, page_of = refs
    count = len(ends)
    size, dim = total.shape[1:]
    place = lax.axis_index("seq")
    places = [place ^ offset for offset in range(count)]
    whole, half = read_logs(ends, size, heads)
    for source in range(count):
        logs_ref[source] = whole[source]
        first_ref[source] = half[source]
    own_pages(owner_ref, place, page_of)

    def fill(slot, carry):
        page = page_of[slot + first]

        @pl.when(page >= 0)
        def _():
            until = page // 2 + page % 2
            logs = [logs_ref[source] for source in range(count)]
            extra = jnp.zeros((heads, dim), jnp.float32)
            for source in range(count):
                extra = extra + jnp.where((places[source] == until) & (page % 2 == 0), first_ref[source], 0.0)
            gather_states(total.at[slot], ends, places, logs, until, extra, heads, dim)

        @pl.when(page < 0)
        def _():
            total[slot] = jnp.zeros((size, dim), jnp.float32)

        return carry

    lax.fori_loop(0, total.shape[0], fill, 0)


def run_reach(page_owner, ends, heads, first, slots):
    count = len(ends)
    rows, dim = ends[0].shape
    size = rows - 6 * heads
    return pl.pallas_call(
        functools.partial(reach_kernel, heads, first),
        in_specs=[SMEM] + [VMEM] * count,
        out_specs=VMEM,
        out_shape=pltpu.VMEM((slots, size, dim), jnp.float32),
        scratch_shapes=[
            pltpu.VMEM((count, heads, dim), jnp.float32),
            pltpu.VMEM((count, heads, dim), jnp.float32),
            pltpu.SMEM((SLOTS,), jnp.int32),
        ],
        compiler_params=pltpu.CompilerParams(vmem_limit_bytes=8 * MIB),
        cost_estimate=SMALL,
        name="reach",
    )(page_owner, *ends)


def cache_kernel(count, owner_ref, *refs):
    mids, totals = refs[:count], refs[count:-4]
    cache_hbm, made, page_of, sems = refs[-4:]
    place = lax.axis_index("seq")
    places = [place ^ offset for offset in range(count)]
    own_pages(owner_ref, place, page_of)
    parts = [(total, slot) for total in totals for slot in range(total.shape[0])]
    copies = []
    for slot, (total, row) in enumerate(parts):
        page = page_of[slot]
        halfway = (page >= 0) & (page % 2 == 0)

        @pl.when(jnp.logical_not(halfway))
        def _():
            made[slot] = total[row].astype(jnp.bfloat16)

        for source in range(count):

            @pl.when(halfway & (places[source] == page // 2))
            def _():
                made[slot] = (total[row] + mids[source][...].astype(jnp.float32)).astype(jnp.bfloat16)

        copies.append(pltpu.make_async_copy(made.at[slot], cache_hbm.at[slot], sems.at[slot]))
        copies[-1].start()
    for copy in copies:
        copy.wait()


def run_cache(page_owner, mids, totals):
    size, dim = mids[0].shape
    count = len(mids)
    return pl.pallas_call(
        functools.partial(cache_kernel, count),
        in_specs=[SMEM] + [VMEM] * (count + len(totals)),
        out_specs=HBM,
        out_shape=jax.ShapeDtypeStruct((SLOTS, size, dim), jnp.bfloat16),
        scratch_shapes=[
            pltpu.VMEM((SLOTS, size, dim), jnp.bfloat16),
            pltpu.SMEM((SLOTS,), jnp.int32),
            pltpu.SemaphoreType.DMA((SLOTS,)),
        ],
        compiler_params=pltpu.CompilerParams(vmem_limit_bytes=8 * MIB),
        cost_estimate=SMALL,
        name="cache",
    )(page_owner, *mids, *totals)


def swap(value, axis, offset):
    return lax.ppermute(value, axis, [(place, place ^ offset) for place in range(lax.axis_size(axis))])


def tie(value, *after):
    return lax.optimization_barrier((value, *after))[0]


def add_kernel(one_ref, two_ref, sum_ref):
    sum_ref[...] = one_ref[...] + two_ref[...]


def add(one, two):
    return pl.pallas_call(
        add_kernel,
        in_specs=[VMEM, VMEM],
        out_specs=VMEM,
        out_shape=pltpu.VMEM(one.shape, one.dtype),
        compiler_params=pltpu.CompilerParams(vmem_limit_bytes=4 * MIB),
        cost_estimate=SMALL,
        name="add",
    )(one, two)


def shards(queries, key_rows, value_rows, decay_log, norm_gain, page_owner):
    tokens, width = queries.shape
    heads = decay_log.shape[0]
    dim = width // heads
    count = lax.axis_size("seq")
    cumulative, states, reached, end, mid, keys, values = run_states(key_rows, value_rows, decay_log)
    held = pltpu.with_memory_space_constraint(tie(queries, cumulative), pltpu.VMEM)
    ends, mids = {0: end}, {0: mid}
    for offset in range(2, count, 2):
        ends[offset] = swap(end, "seq", offset)
    ends[1] = swap(end, "seq", 1)
    mids[1] = swap(mid, "seq", 1)
    inner, grown, done = run_inner(keys, values, held, cumulative, states, reached)
    mid = tie(mid, done, ends[1], mids[1])
    for offset in range(2, count, 2):
        mids[offset] = swap(mid, "seq", offset)
    for offset in range(2, count, 2):
        ends[offset + 1] = swap(tie(ends[offset], done), "seq", 1)
    ends = [ends[offset] for offset in range(count)]
    out, square = run_finish(inner, grown, norm_gain, ends, heads)
    totals = []
    shares = [(0, 3), (3, SLOTS - 3)]
    offset = 1
    while offset < lax.axis_size("head"):
        other = swap(square, "head", offset)
        if shares:
            totals.append(run_reach(tie(page_owner, square), ends, heads, *shares.pop(0)))
            other = tie(other, totals[-1])
        square = add(square, other)
        if offset == 1:
            for part in range(2, count, 2):
                if part != count - 2:
                    mids[part + 1] = swap(tie(mids[part], square), "seq", 1)
        offset *= 2
    for first, slots in shares:
        totals.append(run_reach(tie(page_owner, square), ends, heads, first, slots))
    mids[count - 1] = swap(tie(mids[count - 2], square), "seq", 1)
    mids = [mids[offset] for offset in range(count)]
    attended = run_scale(out, square, width * lax.axis_size("head"))
    page_cache = run_cache(page_owner, mids, totals)
    return attended, page_cache.reshape(SLOTS, heads, dim, dim)


def solution(mesh):
    return jax.shard_map(
        shards,
        mesh=mesh,
        in_specs=(
            P("seq", "head"),
            P("seq", "head"),
            P("seq", "head"),
            P("head", "seq"),
            P("head"),
            P(),
        ),
        out_specs=(P("seq", "head"), P("seq", "head", None, None)),
        check_vma=False,
    )
```

```python
import functools
import math

import jax
import jax.numpy as jnp
from jax import lax
from jax.experimental import pallas as pl
from jax.experimental.pallas import tpu as pltpu
from jax.sharding import PartitionSpec as P

BLOCK = 256
ROWS = 512
PAGE = 1024
SLOTS = 5
LOG2E = math.log2(math.e)
MIB = 1 << 20
SMALL = pl.CostEstimate(flops=1, bytes_accessed=1, transcendentals=0)

NT = (((1,), (1,)), ((), ()))
TN = (((0,), (0,)), ((), ()))


def split3(x):
    high = x.astype(jnp.bfloat16)
    rest = x - high.astype(jnp.float32)
    middle = rest.astype(jnp.bfloat16)
    low = (rest - middle.astype(jnp.float32)).astype(jnp.bfloat16)
    return high, middle, low


def state_kernel(heads, key_hbm, value_hbm, decay_hbm, cum_ref, states_ref, reached_ref, end_ref, mid_ref, keys, values, decays, running, sems):
    tokens, width = keys.shape
    dim = width // heads
    size = heads * dim
    blocks = tokens // BLOCK
    decay_copy = pltpu.make_async_copy(decay_hbm, decays, sems.at[2 * blocks])
    decay_copy.start()
    copies = []
    for blk in range(blocks):
        rows = pl.ds(blk * BLOCK, BLOCK)
        copies.append(
            (
                pltpu.make_async_copy(key_hbm.at[rows], keys.at[rows], sems.at[2 * blk]),
                pltpu.make_async_copy(value_hbm.at[rows], values.at[rows], sems.at[2 * blk + 1]),
            )
        )
        copies[-1][0].start()
        copies[-1][1].start()
    upper = jnp.where(
        lax.broadcasted_iota(jnp.int32, (BLOCK, BLOCK), 0) <= lax.broadcasted_iota(jnp.int32, (BLOCK, BLOCK), 1), 1.0, 0.0
    ).astype(jnp.bfloat16)
    decay_copy.wait()
    parts = [
        part for blk in range(blocks) for part in split3(decays[:, blk * BLOCK : (blk + 1) * BLOCK] * LOG2E)
    ]
    sums = jnp.dot(jnp.concatenate(parts, axis=0), upper, preferred_element_type=jnp.float32)
    to_last, decay = [], []
    reached = jnp.zeros((heads, dim), jnp.float32)
    for blk in range(blocks):
        base = 3 * heads * blk
        cum = sums[base : base + heads] + sums[base + heads : base + 2 * heads] + sums[base + 2 * heads : base + 3 * heads]
        cum_ref[:, blk * BLOCK : (blk + 1) * BLOCK] = cum
        last = cum[:, BLOCK - 1 :]
        to_last.append(jnp.exp2(last - cum))
        wide = jnp.broadcast_to(last, (heads, dim))
        decay.append(jnp.exp2(wide))
        reached = reached + wide
        reached_ref[blk] = reached
        if blk == PAGE // BLOCK - 1:
            end_ref[size + 3 * heads :] = jnp.concatenate(split3(reached), axis=0)
    end_ref[size : size + 3 * heads] = jnp.concatenate(split3(reached), axis=0)
    for blk in range(blocks):
        copies[blk][0].wait()
        copies[blk][1].wait()
        here = slice(blk * BLOCK, (blk + 1) * BLOCK)
        for pair in range(heads // 2):
            scaled = []
            for head in (2 * pair, 2 * pair + 1):
                turned = keys[here, head * dim : (head + 1) * dim].T.astype(jnp.float32)
                scaled.append((turned * to_last[blk][head : head + 1]).astype(jnp.bfloat16))
            update = jnp.dot(
                jnp.concatenate(scaled, axis=0),
                values[here, 2 * pair * dim : 2 * (pair + 1) * dim],
                preferred_element_type=jnp.float32,
            )
            for which, head in enumerate((2 * pair, 2 * pair + 1)):
                rows = slice(head * dim, (head + 1) * dim)
                cols = slice(which * dim, (which + 1) * dim)
                state = update[cols, cols]
                if blk:
                    state = state + decay[blk][head : head + 1] * running[rows]
                running[rows] = state
                states_ref[blk, rows] = state.astype(jnp.bfloat16)
                if blk == PAGE // BLOCK - 1:
                    mid_ref[rows] = state.astype(jnp.bfloat16)
                if blk == blocks - 1:
                    end_ref[rows] = state.astype(jnp.bfloat16)


def in_hbm(value):
    return pltpu.with_memory_space_constraint(value, pltpu.HBM)


HBM = pl.BlockSpec(memory_space=pltpu.HBM)
VMEM = pl.BlockSpec(memory_space=pltpu.VMEM)
SMEM = pl.BlockSpec(memory_space=pltpu.SMEM)


def run_states(key_rows, value_rows, decay_log):
    tokens, width = key_rows.shape
    heads = decay_log.shape[0]
    dim = width // heads
    blocks = tokens // BLOCK
    size = heads * dim
    return pl.pallas_call(
        functools.partial(state_kernel, heads),
        in_specs=[HBM] * 3,
        out_specs=[VMEM] * 7,
        out_shape=[
            pltpu.VMEM((heads, tokens), jnp.float32),
            pltpu.VMEM((blocks, size, dim), jnp.bfloat16),
            pltpu.VMEM((blocks, heads, dim), jnp.float32),
            pltpu.VMEM((size + 6 * heads, dim), jnp.bfloat16),
            pltpu.VMEM((size, dim), jnp.bfloat16),
            pltpu.VMEM((tokens, width), jnp.bfloat16),
            pltpu.VMEM((tokens, width), jnp.bfloat16),
        ],
        scratch_shapes=[
            pltpu.VMEM((heads, tokens), jnp.float32),
            pltpu.VMEM((size, dim), jnp.float32),
            pltpu.SemaphoreType.DMA((2 * blocks + 1,)),
        ],
        compiler_params=pltpu.CompilerParams(vmem_limit_bytes=8 * MIB),
        cost_estimate=SMALL,
        name="states",
    )(in_hbm(key_rows), in_hbm(value_rows), in_hbm(decay_log))


def pair_of(one, two):
    zero = jnp.zeros_like(one)
    return jnp.concatenate([jnp.concatenate([one, zero], axis=1), jnp.concatenate([zero, two], axis=1)], axis=0)


def inner_kernel(heads, keys, values, queries, cum_ref, states_ref, reached_ref, out_ref, grown_ref, done_ref):
    step = pl.program_id(0)
    width = queries.shape[1]
    dim = width // heads
    causal = lax.broadcasted_iota(jnp.int32, (BLOCK, BLOCK), 0) >= lax.broadcasted_iota(jnp.int32, (BLOCK, BLOCK), 1)
    blks = [step * (ROWS // BLOCK) + part for part in range(ROWS // BLOCK)]
    here = [pl.ds(pl.multiple_of(blk * BLOCK, BLOCK), BLOCK) for blk in blks]
    before = [jnp.maximum(blk, 1) - 1 for blk in blks]
    cums = [cum_ref[:, rows] for rows in here]
    cum_cols = [cum.T for cum in cums]
    reached = [jnp.where(blk > 0, reached_ref[last], 0.0) for blk, last in zip(blks, before)]
    items = [(pair + which, part) for pair in range(0, heads, 2) for part in range(len(blks)) for which in range(2)]

    def scores_of(head, part):
        lanes = slice(head * dim, (head + 1) * dim)
        return lax.dot_general(queries[here[part], lanes], keys[here[part], lanes], NT, preferred_element_type=jnp.float32)

    def carried_of(pair, part):
        states = []
        for head in (2 * pair, 2 * pair + 1):
            state = states_ref[before[part], head * dim : (head + 1) * dim]
            states.append(jnp.where(blks[part] > 0, state, jnp.zeros_like(state)))
        query = queries[here[part], 2 * pair * dim : 2 * (pair + 1) * dim]
        return jnp.dot(query, pair_of(*states), preferred_element_type=jnp.float32)

    scores = scores_of(*items[0])
    carried = {}
    for number, (head, part) in enumerate(items):
        ahead = scores_of(*items[number + 1]) if number + 1 < len(items) else None
        if head % 2 == 0:
            carried[part] = carried_of(head // 2, part)
        lanes = slice(head * dim, (head + 1) * dim)
        column = jnp.broadcast_to(cum_cols[part][:, head : head + 1], (BLOCK, dim))
        columns = jnp.concatenate([column] * (BLOCK // dim), axis=1)
        weights = jnp.where(causal, scores * jnp.exp2(columns - cums[part][head : head + 1]), 0.0)
        local = jnp.dot(weights.astype(jnp.bfloat16), values[here[part], lanes], preferred_element_type=jnp.float32)
        which = head % 2
        local = local + carried[part][:, which * dim : (which + 1) * dim] * jnp.exp2(column)
        out_ref[here[part], lanes] = local
        growth = jnp.exp2(column + reached[part][head : head + 1])
        grown_ref[here[part], lanes] = (queries[here[part], lanes].astype(jnp.float32) * growth).astype(jnp.bfloat16)
        scores = ahead
    done_ref[...] = cums[0][:, :128]


def run_inner(keys, values, queries, cumulative, states, reached):
    tokens, width = keys.shape
    heads = cumulative.shape[0]
    made = pltpu.VMEM((tokens, width), jnp.float32)
    return pl.pallas_call(
        functools.partial(inner_kernel, heads),
        grid=(tokens // ROWS,),
        in_specs=[VMEM] * 6,
        out_specs=[VMEM] * 3,
        out_shape=[made, pltpu.VMEM((tokens, width), jnp.bfloat16), pltpu.VMEM((heads, 128), jnp.float32)],
        compiler_params=pltpu.CompilerParams(vmem_limit_bytes=8 * MIB),
        cost_estimate=SMALL,
        name="inner",
    )(keys, values, queries, cumulative, states, reached)


def read_logs(ends, size, heads):
    whole, first = [], []
    for end in ends:
        parts = end[size:].astype(jnp.float32)
        whole.append(parts[:heads] + parts[heads : 2 * heads] + parts[2 * heads : 3 * heads])
        first.append(parts[3 * heads : 4 * heads] + parts[4 * heads : 5 * heads] + parts[5 * heads :])
    return whole, first


def gather_states(total, ends, places, logs, place, extra, heads, dim):
    factors = []
    for source in range(len(ends)):
        log = extra
        for other, other_log in enumerate(logs):
            between = (places[other] > places[source]) & (places[other] < place)
            log = log + jnp.where(between, other_log, 0.0)
        factors.append(jnp.where(places[source] < place, jnp.exp2(log), 0.0))
    for head in range(heads):
        rows = slice(head * dim, (head + 1) * dim)
        value = jnp.zeros((dim, dim), jnp.float32)
        for source, end in enumerate(ends):
            value += factors[source][head : head + 1] * end[rows].astype(jnp.float32)
        total[rows] = value


def finish_kernel(heads, inner_ref, grown, gain_ref, *refs):
    *ends, out_ref, square_ref, entry, entry_low = refs
    blk = pl.program_id(0)
    tokens, width = grown.shape
    length = PAGE
    dim = width // heads
    size = heads * dim

    @pl.when(blk == 0)
    def _():
        place = lax.axis_index("seq")
        logs, _unused = read_logs(ends, size, heads)
        places = [place ^ offset for offset in range(len(ends))]
        gather_states(entry, ends, places, logs, place, jnp.zeros((heads, dim), jnp.float32), heads, dim)
        entry_low[...] = entry[...].astype(jnp.bfloat16)

    here = pl.ds(pl.multiple_of(blk * length, length), length)

    def carried_of(pair):
        rows = [slice(head * dim, (head + 1) * dim) for head in (2 * pair, 2 * pair + 1)]
        query = grown[here, 2 * pair * dim : 2 * (pair + 1) * dim]
        return jnp.dot(query, pair_of(entry_low[rows[0]], entry_low[rows[1]]), preferred_element_type=jnp.float32)

    total = jnp.zeros((length, dim), jnp.float32)
    ahead = carried_of(0)
    for pair in range(heads // 2):
        carried = ahead
        if pair + 1 < heads // 2:
            ahead = carried_of(pair + 1)
        lanes = slice(2 * pair * dim, 2 * (pair + 1) * dim)
        out = inner_ref[here, lanes] + carried
        squares = out * out
        total += squares[:, :dim] + squares[:, dim:]
        out_ref[here, lanes] = out * gain_ref[:, lanes]
    high = total.astype(jnp.bfloat16)
    low = (total - high.astype(jnp.float32)).astype(jnp.bfloat16)
    ones = jnp.ones((8, dim), jnp.bfloat16)
    sums = lax.dot_general(ones, high, NT, preferred_element_type=jnp.float32)
    sums = sums + lax.dot_general(ones, low, NT, preferred_element_type=jnp.float32)
    for row in range(length // 128):
        square_ref[pl.ds(blk * (length // 128) + row, 1)] = sums[:1, row * 128 : (row + 1) * 128]


def run_finish(inner, grown, gain, ends, heads):
    tokens, width = grown.shape
    dim = width // heads
    size = heads * dim
    return pl.pallas_call(
        functools.partial(finish_kernel, heads),
        grid=(tokens // PAGE,),
        in_specs=[VMEM] * (3 + len(ends)),
        out_specs=[VMEM, VMEM],
        out_shape=[pltpu.VMEM((tokens, width), jnp.float32), pltpu.VMEM((tokens // 128, 128), jnp.float32)],
        scratch_shapes=[pltpu.VMEM((size, dim), jnp.float32), pltpu.VMEM((size, dim), jnp.bfloat16)],
        compiler_params=pltpu.CompilerParams(vmem_limit_bytes=8 * MIB),
        cost_estimate=SMALL,
        name="finish",
    )(inner, grown, gain.reshape(1, width), *ends)


def scale_kernel(whole_width, out_ref, square, attended_hbm, made, sems):
    blk = pl.program_id(0)
    tokens, width = made.shape

    def copy_of(part):
        rows = pl.ds(part * BLOCK, BLOCK)
        return pltpu.make_async_copy(made.at[rows], attended_hbm.at[rows], sems.at[part])

    for sub in range(ROWS // BLOCK):
        base = blk * ROWS + sub * BLOCK
        scales = []
        for part in range(BLOCK // 128):
            total = square[pl.ds(blk * (ROWS // 128) + sub * (BLOCK // 128) + part, 1)]
            scale = lax.rsqrt(total * (1.0 / whole_width) + 1e-06)
            scales.append(jnp.broadcast_to(jnp.broadcast_to(scale, (8, 128)).T[:, :1], (128, 128)))
        scale = jnp.concatenate(scales, axis=0)
        here = pl.ds(pl.multiple_of(base, BLOCK), BLOCK)
        for col in range(0, width, 128):
            made[here, col : col + 128] = (out_ref[here, col : col + 128] * scale).astype(jnp.bfloat16)
        for step in range(tokens // ROWS):

            @pl.when(blk == step)
            def _():
                copy_of(step * (ROWS // BLOCK) + sub).start()

    @pl.when(blk == pl.num_programs(0) - 1)
    def _():
        for part in range(tokens // BLOCK):
            copy_of(part).wait()


def run_scale(out, square, whole_width):
    tokens, width = out.shape
    return pl.pallas_call(
        functools.partial(scale_kernel, whole_width),
        grid=(tokens // ROWS,),
        in_specs=[VMEM] * 2,
        out_specs=HBM,
        out_shape=jax.ShapeDtypeStruct((tokens, width), jnp.bfloat16),
        scratch_shapes=[pltpu.VMEM((tokens, width), jnp.bfloat16), pltpu.SemaphoreType.DMA((tokens // BLOCK,))],
        compiler_params=pltpu.CompilerParams(vmem_limit_bytes=12 * MIB),
        cost_estimate=SMALL,
        name="scale",
    )(out, square)


def own_pages(owner_ref, place, page_of):
    for slot in range(SLOTS):
        page_of[slot] = -1

    def look(page, found):
        mine = (owner_ref[page] == place) & (found < SLOTS)

        @pl.when(mine)
        def _():
            page_of[found] = page

        return found + mine.astype(jnp.int32)

    lax.fori_loop(0, owner_ref.shape[0], look, jnp.int32(0))


def reach_kernel(heads, first, owner_ref, *refs):
    *ends, total, logs_ref, first_ref, page_of = refs
    count = len(ends)
    size, dim = total.shape[1:]
    place = lax.axis_index("seq")
    places = [place ^ offset for offset in range(count)]
    whole, half = read_logs(ends, size, heads)
    for source in range(count):
        logs_ref[source] = whole[source]
        first_ref[source] = half[source]
    own_pages(owner_ref, place, page_of)

    def fill(slot, carry):
        page = page_of[slot + first]

        @pl.when(page >= 0)
        def _():
            until = page // 2 + page % 2
            logs = [logs_ref[source] for source in range(count)]
            extra = jnp.zeros((heads, dim), jnp.float32)
            for source in range(count):
                extra = extra + jnp.where((places[source] == until) & (page % 2 == 0), first_ref[source], 0.0)
            gather_states(total.at[slot], ends, places, logs, until, extra, heads, dim)

        @pl.when(page < 0)
        def _():
            total[slot] = jnp.zeros((size, dim), jnp.float32)

        return carry

    lax.fori_loop(0, total.shape[0], fill, 0)


def run_reach(page_owner, ends, heads, first, slots):
    count = len(ends)
    rows, dim = ends[0].shape
    size = rows - 6 * heads
    return pl.pallas_call(
        functools.partial(reach_kernel, heads, first),
        in_specs=[SMEM] + [VMEM] * count,
        out_specs=VMEM,
        out_shape=pltpu.VMEM((slots, size, dim), jnp.float32),
        scratch_shapes=[
            pltpu.VMEM((count, heads, dim), jnp.float32),
            pltpu.VMEM((count, heads, dim), jnp.float32),
            pltpu.SMEM((SLOTS,), jnp.int32),
        ],
        compiler_params=pltpu.CompilerParams(vmem_limit_bytes=8 * MIB),
        cost_estimate=SMALL,
        name="reach",
    )(page_owner, *ends)


def cache_kernel(paired, count, owner_ref, *refs):
    mids, totals = refs[:count], refs[count:-4]
    cache_hbm, made, page_of, sems = refs[-4:]
    place = lax.axis_index("seq")
    size = made.shape[1]
    if paired:
        odd = place % 2 == 1
        chips = [place, place ^ jnp.where(odd, 4, 2), place ^ jnp.where(odd, 2, 4)]
        sources = [
            (mids[number], core * size, chip - chip % 2 + core) for number, chip in enumerate(chips) for core in range(2)
        ]
        sources += [(mids[3], 0, place ^ 6), (mids[4], 0, place ^ 7)]
    else:
        sources = [(mids[offset], 0, place ^ offset) for offset in range(count)]
    own_pages(owner_ref, place, page_of)
    parts = [(total, slot) for total in totals for slot in range(total.shape[0])]
    copies = []
    for slot, (total, row) in enumerate(parts):
        page = page_of[slot]
        halfway = (page >= 0) & (page % 2 == 0)

        @pl.when(jnp.logical_not(halfway))
        def _():
            made[slot] = total[row].astype(jnp.bfloat16)

        for source, start, owner in sources:

            @pl.when(halfway & (owner == page // 2))
            def _():
                made[slot] = (total[row] + source[start : start + size].astype(jnp.float32)).astype(jnp.bfloat16)

        copies.append(pltpu.make_async_copy(made.at[slot], cache_hbm.at[slot], sems.at[slot]))
        copies[-1].start()
    for copy in copies:
        copy.wait()


def run_cache(page_owner, mids, totals, paired):
    size, dim = totals[0].shape[1:]
    count = len(mids)
    return pl.pallas_call(
        functools.partial(cache_kernel, paired, count),
        in_specs=[SMEM] + [VMEM] * (count + len(totals)),
        out_specs=HBM,
        out_shape=jax.ShapeDtypeStruct((SLOTS, size, dim), jnp.bfloat16),
        scratch_shapes=[
            pltpu.VMEM((SLOTS, size, dim), jnp.bfloat16),
            pltpu.SMEM((SLOTS,), jnp.int32),
            pltpu.SemaphoreType.DMA((SLOTS,)),
        ],
        compiler_params=pltpu.CompilerParams(vmem_limit_bytes=8 * MIB),
        cost_estimate=SMALL,
        name="cache",
    )(page_owner, *mids, *totals)


def swap(value, axis, offset):
    return lax.ppermute(value, axis, [(place, place ^ offset) for place in range(lax.axis_size(axis))])


def pack_kernel(mine_ref, other_ref, both_ref):
    core = lax.axis_index("seq") % 2
    size = mine_ref.shape[0]
    both_ref[pl.ds(pl.multiple_of(core * size, size), size)] = mine_ref[...]
    both_ref[pl.ds(pl.multiple_of((1 - core) * size, size), size)] = other_ref[...]


def pack(mine, other):
    return pl.pallas_call(
        pack_kernel,
        in_specs=[VMEM, VMEM],
        out_specs=VMEM,
        out_shape=pltpu.VMEM((2 * mine.shape[0], mine.shape[1]), mine.dtype),
        compiler_params=pltpu.CompilerParams(vmem_limit_bytes=4 * MIB),
        cost_estimate=SMALL,
        name="pack",
    )(mine, other)


def tie(value, *after):
    return lax.optimization_barrier((value, *after))[0]


def add_kernel(one_ref, two_ref, sum_ref):
    sum_ref[...] = one_ref[...] + two_ref[...]


def add(one, two):
    return pl.pallas_call(
        add_kernel,
        in_specs=[VMEM, VMEM],
        out_specs=VMEM,
        out_shape=pltpu.VMEM(one.shape, one.dtype),
        compiler_params=pltpu.CompilerParams(vmem_limit_bytes=4 * MIB),
        cost_estimate=SMALL,
        name="add",
    )(one, two)


def shards(queries, key_rows, value_rows, decay_log, norm_gain, page_owner):
    tokens, width = queries.shape
    heads = decay_log.shape[0]
    dim = width // heads
    count = lax.axis_size("seq")
    cumulative, states, reached, end, mid, keys, values = run_states(key_rows, value_rows, decay_log)
    held = pltpu.with_memory_space_constraint(tie(queries, cumulative), pltpu.VMEM)
    ends, mids = {0: end}, {0: mid}
    for offset in range(2, count, 2):
        ends[offset] = swap(end, "seq", offset)
    ends[1] = swap(end, "seq", 1)
    mids[1] = swap(mid, "seq", 1)
    inner, grown, done = run_inner(keys, values, held, cumulative, states, reached)
    paired = count == 8
    if paired:
        both = pack(mid, mids[1])
        crossed = lax.ppermute(both, "seq", [(place, place ^ (4 if place % 2 else 2)) for place in range(count)])
        far = swap(mid, "seq", 6)
    else:
        for offset in range(2, count, 2):
            mids[offset] = swap(mid, "seq", offset)
    for offset in range(2, count, 2):
        ends[offset + 1] = swap(tie(ends[offset], done), "seq", 1)
    ends = [ends[offset] for offset in range(count)]
    out, square = run_finish(inner, grown, norm_gain, ends, heads)
    totals = []
    shares = [(0, 3), (3, SLOTS - 3)]
    offset = 1
    while offset < lax.axis_size("head"):
        other = swap(square, "head", offset)
        if shares:
            totals.append(run_reach(tie(page_owner, square), ends, heads, *shares.pop(0)))
            other = tie(other, totals[-1])
        square = add(square, other)
        if offset == 1 and paired:
            crossed_other = swap(tie(crossed, square), "seq", 1)
        offset *= 2
    for first, slots in shares:
        totals.append(run_reach(tie(page_owner, square), ends, heads, first, slots))
    if paired:
        mids = [both, crossed, crossed_other, far, swap(tie(far, square), "seq", 1)]
    else:
        for offset in range(2, count, 2):
            mids[offset + 1] = swap(mids[offset], "seq", 1)
        mids = [mids[offset] for offset in range(count)]
    attended = run_scale(out, square, width * lax.axis_size("head"))
    page_cache = run_cache(page_owner, mids, totals, paired)
    return attended, page_cache.reshape(SLOTS, heads, dim, dim)


def solution(mesh):
    return jax.shard_map(
        shards,
        mesh=mesh,
        in_specs=(
            P("seq", "head"),
            P("seq", "head"),
            P("seq", "head"),
            P("head", "seq"),
            P("head"),
            P(),
        ),
        out_specs=(P("seq", "head"), P("seq", "head", None, None)),
        check_vma=False,
    )
```
